128 devices in a mesh: occi: 8 (over y, core), occj: 16 (over z, x).
Axes of the slice: x: 4, y: 4, z: 4, core: 2. Of those that a mesh axis runs over, the one named last changes fastest.
Arguments:
- factors: float32 [128, 512, 256], P(('occi', 'occj')), may hold values from -6 to 6
- pno_vecs: float32 [8192, 256, 128], P(('occi', 'occj')), may hold values from -0.09375 to 0.09375
- pair_occ: int32 [8192, 2], P(('occi', 'occj')), may hold values from 0 to 127, as said below
- pno_count: int32 [8192], P(('occi', 'occj')), may hold values from 32 to 128, as said below
- pno_energy: float32 [8192, 128], P(('occi', 'occj')), may hold values from 0.3 to 3
- occ_energy: float32 [128], replicated, may hold values from -1.5 to -0.3
- coupi_peer: int32 [4096, 1], P(('occi', 'occj')), may hold values from 0 to 7; in each aligned block of 32 rows (0 to 31, 32 to 63, ...) at most 8 rows name the same one
- coupi_slot: int32 [4096], P(('occi', 'occj')), may hold values from 0 to 63
- coupi_target: int32 [4096], P(('occi', 'occj')), may hold values from 0 to 63
- coupi_fock: float32 [4096], P(('occi', 'occj')), may hold values from -0.5 to 0.5
- coupi_correlation: float32 [4096, 128, 128], P(('occi', 'occj')), may hold values from -0.15 to 1, as said below
- coupj_peer: int32 [4096, 1], P(('occi', 'occj')), may hold values from 0 to 15; in each aligned block of 32 rows (0 to 31, 32 to 63, ...) at most 4 rows name the same one
- coupj_slot: int32 [4096], P(('occi', 'occj')), may hold values from 0 to 63
- coupj_target: int32 [4096], P(('occi', 'occj')), may hold values from 0 to 63
- coupj_fock: float32 [4096], P(('occi', 'occj')), may hold values from -0.5 to 0.5
- coupj_correlation: float32 [4096, 128, 128], P(('occi', 'occj')), may hold values from -0.15 to 1, as said below
Outputs:
- amplitude: float32 [8192, 128, 128], P(('occi', 'occj'))
- residual: float32 [8192, 128, 128], P(('occi', 'occj'))
The draws below stay inside these ranges and needn't reach their ends.
Inputs may be any that keep to these rules, and one draw needn't show every extreme that they name: `pair_occ`: the pairs in the rows of one device have their first orbital in that device's occi block of 1 * 16 orbitals starting at u * 16, and their second orbital o in its occj block: (o) % 16 equals the device's occj index. `pno_count`: pair 0 uses all 128 natural orbitals. `coupi_peer`: in the rows of one device no peer index appears more than 8 times. `coupj_peer`: in the rows of one device no peer index appears more than 4 times. `coupi_correlation`: diagonal entries lie in 0.5 to 1. `coupj_correlation`: diagonal entries lie in 0.5 to 1.
All inputs are finite; a program needn't handle non-finite values.
Results may differ from the reference program's by a relative error of at most 0.0003.
Values sent between devices are 32-bit elements; how exact they have to be, the bound alone decides.
A program may use at most 128 MiB of HBM per device.

```python
import math
import jax
import jax.numpy as jnp
import numpy as np
from jax import lax

NAUX = 512
NVIR = 256
NPNO = 128
OCC_DEV = 1
PAIRS_DEV = 64
COUPI_DEV = 32
COUPJ_DEV = 32
ITERS = 2
CAPI = 8
CAPJ = 4
NOCC = 128
PAIRS = 8192
COUPI = 4096
COUPJ = 4096
N_OCCI = 8
N_OCCJ = 16


def draw_pair_occ(key, part):
    device_count = N_OCCI * N_OCCJ
    block_first = OCC_DEV * N_OCCJ
    block_second = OCC_DEV * N_OCCI
    cell_count = block_first * block_second
    repeats = (PAIRS_DEV + cell_count - 1) // cell_count
    device_keys = jax.random.split(jax.random.fold_in(key, 11), device_count)

    def choose(device_key):
        shuffled = jax.random.permutation(device_key, cell_count * repeats)
        return shuffled[:PAIRS_DEV] % cell_count
    chosen = jax.vmap(choose)(device_keys)
    device = jnp.arange(device_count)[:, None]
    first_block = device // N_OCCJ
    second_block = device % N_OCCJ
    row_first = chosen // block_second
    row_second = chosen % block_second
    occ_first = first_block * block_first + row_first
    occ_second = (row_second // OCC_DEV * N_OCCJ + second_block) * OCC_DEV + row_second % OCC_DEV
    return jnp.stack([occ_first, occ_second], -1).reshape(device_count * PAIRS_DEV, 2).astype(jnp.int32)


def draw_pno_count(key, part):
    counts = jax.random.randint(jax.random.fold_in(key, 13), (PAIRS_DEV * N_OCCI * N_OCCJ,), NPNO // 4, NPNO + 1)
    return counts.at[0].set(NPNO).astype(jnp.int32)


def correlation_draw(key, count):
    diagonal = jax.random.uniform(jax.random.fold_in(key, 1), (count, NPNO), jnp.float32, 0.5, 1.0)
    spread = jnp.clip(0.03 * jax.random.normal(jax.random.fold_in(key, 2), (count, NPNO, NPNO), jnp.float32), -0.15, 0.15)
    eye = jnp.eye(NPNO, dtype=jnp.float32)
    return (spread * (1.0 - eye) + diagonal[:, :, None] * eye).astype(jnp.float32)


def draw_coupi_correlation(key, part):
    return correlation_draw(jax.random.fold_in(key, 21), COUPI_DEV * N_OCCI * N_OCCJ)


def draw_coupj_correlation(key, part):
    return correlation_draw(jax.random.fold_in(key, 23), COUPJ_DEV * N_OCCI * N_OCCJ)


def with_ends(array, own_key, least, top_value):
    place = [jax.random.randint(jax.random.fold_in(own_key, axis), (), 0, length) for axis, length in enumerate(array.shape)]
    longest = array.shape.index(max(array.shape))
    neighbour = place[:longest] + [(place[longest] + 1) % array.shape[longest]] + place[longest + 1:]
    return array.at[tuple(place)].set(least).at[tuple(neighbour)].set(top_value)


def shard_levels(key, extent, shards, least, largest):
    factor_of = 1.0
    for axis_at, parts in shards:
        steps = jax.random.uniform(jax.random.fold_in(jax.random.fold_in(key, 6), axis_at), (parts,), jnp.float32, least / len(shards), largest / len(shards))
        factor_of = factor_of * jnp.repeat(jnp.exp(steps), extent[axis_at] // parts).reshape((-1,) + (1,) * (len(extent) - 1 - axis_at))
    return factor_of


def shared_out(rng, own, number, rows, number_of, top, bound, skew):
    ranking = jax.random.permutation(rng, number_of)
    heavy_load, common = load_shares(number_of, rows * top, bound, skew, True), load_shares(number_of, rows * top, bound, skew, False)
    places = jnp.arange(number_of)

    def named(tallies, turn):
        used = int((tallies > 0).sum())
        fixed = max(1, used // 4)
        shifted = fixed + (places - fixed + turn * (used - fixed)) % max(1, number_of - fixed)
        return jnp.zeros((number_of,), jnp.int32).at[ranking[jnp.where(places < fixed, places, shifted)]].set(jnp.asarray(tallies, jnp.int32))

    tallies = jnp.where(number % 4 == 0, named(heavy_load, number // 4), named(common, number - number // 4 - 1))
    mixed = jax.random.permutation(jax.random.fold_in(own, 3), number_of)
    source_of, receiver = mixed[0:number_of // 2 * 2:2], mixed[1:number_of // 2 * 2:2]
    room = jnp.minimum(tallies[source_of] - 1, bound - tallies[receiver]) // 2
    room = jnp.where((source_of == ranking[0]) | (receiver == ranking[0]) | (tallies[receiver] == 0), 0, jnp.maximum(room, 0))
    shifted = jax.random.randint(jax.random.fold_in(own, 4), (number_of // 2,), 0, 1 << 20) % (room + 1)
    tallies = tallies.at[source_of].add(-shifted).at[receiver].add(shifted)
    members = jnp.searchsorted(jnp.cumsum(tallies), jnp.arange(rows * top), side="right").astype(jnp.int32)
    listing = members.reshape(top, rows).T
    listing = listing[jax.random.permutation(jax.random.fold_in(own, 1), rows)]
    turn = jax.random.randint(jax.random.fold_in(own, 2), (rows, 1), 0, top)
    return jnp.take_along_axis(listing, (jnp.arange(top)[None, :] + turn) % top, axis=1)


def load_shares(count, total, most, slope, full):
    loads = [(1 << 20) // math.isqrt(grade ** slope) + 1 for grade in range(1, count + 1)]
    largest = most if full else min(most, max(-(-total // count), total * loads[0] // sum(loads)))
    least = 1 if total - largest >= count - 1 else 0
    holding, spare = [largest] + [least] * (count - 1), total - largest - least * (count - 1)
    while spare > 0:
        free = [i for i in range(1, count) if holding[i] < largest] or [i for i in range(1, count) if holding[i] < most]
        whole, remaining = sum([loads[i] for i in free]), spare
        for i in free:
            extra = min(most - holding[i], max(1, remaining * loads[i] // whole), spare)
            holding[i] = holding[i] + extra
            spare = spare - extra
    return np.array(holding)


def normal_values(key, extent, deviation, most, pieces=(), kind=jnp.bfloat16):
    gain = shard_levels(key, extent, pieces, -0.22, 0.18) if pieces else 1.0
    values = jax.random.normal(key, extent, jnp.float32) * deviation * gain
    return jnp.minimum(jnp.maximum(values, -most), most).astype(kind)


def setup_inputs(seed: int = 0) -> dict:
    key_list = jax.random.split(jax.random.key(seed), 17)
    factors = normal_values(key_list[0], (NOCC, NAUX, NVIR), 1.0, 6.0, ((0, 128),), jnp.float32)
    pno_vecs = normal_values(key_list[1], (PAIRS, NVIR, NPNO), (NVIR * 16) ** -0.5, 0.09375, ((0, 128),), jnp.float32)
    pair_occ = draw_pair_occ(jax.random.fold_in(key_list[16], 71), 0)
    pno_count = draw_pno_count(jax.random.fold_in(key_list[16], 71), 0)
    pno_energy = jnp.clip(jnp.exp(math.log(3.0) - 2.3025851 * jax.random.uniform(key_list[4], (PAIRS, NPNO), jnp.float32) ** shard_levels(key_list[4], (PAIRS, NPNO), ((0, 128),), -0.2, 0.2)), 0.3, 3.0)
    occ_energy = jnp.clip(jax.random.uniform(key_list[5], (NOCC,), jnp.float32, -1.5, -0.3), -1.5, -0.3)
    coupi_peer_keys = jax.random.split(jax.random.fold_in(key_list[6], 1), COUPI // COUPI_DEV)
    coupi_peer_turns = jax.random.permutation(jax.random.fold_in(key_list[6], 3), COUPI // COUPI_DEV)
    coupi_peer = jax.vmap(lambda own, number: shared_out(jax.random.fold_in(key_list[6], 2), own, number, COUPI_DEV, N_OCCI, 1, CAPI, 2))(coupi_peer_keys, coupi_peer_turns).reshape((COUPI, 1))
    coupi_slot = with_ends(jax.random.randint(key_list[7], (COUPI,), 0, PAIRS_DEV), jax.random.fold_in(key_list[7], 1), 0, PAIRS_DEV - 1).astype(jnp.int32)
    coupi_target = with_ends(jax.random.randint(key_list[8], (COUPI,), 0, PAIRS_DEV), jax.random.fold_in(key_list[8], 1), 0, PAIRS_DEV - 1).astype(jnp.int32)
    coupi_fock = jnp.clip(jax.random.uniform(key_list[9], (COUPI,), jnp.float32, -0.5, 0.5) * shard_levels(key_list[9], (COUPI,), ((0, 128),), -0.4, 0.0), -0.5, 0.5)
    coupi_correlation = draw_coupi_correlation(jax.random.fold_in(key_list[16], 71), 0)
    coupj_peer_keys = jax.random.split(jax.random.fold_in(key_list[11], 1), COUPJ // COUPJ_DEV)
    coupj_peer_turns = jax.random.permutation(jax.random.fold_in(key_list[11], 3), COUPJ // COUPJ_DEV)
    coupj_peer = jax.vmap(lambda own, number: shared_out(jax.random.fold_in(key_list[11], 2), own, number, COUPJ_DEV, N_OCCJ, 1, CAPJ, 2))(coupj_peer_keys, coupj_peer_turns).reshape((COUPJ, 1))
    coupj_slot = with_ends(jax.random.randint(key_list[12], (COUPJ,), 0, PAIRS_DEV), jax.random.fold_in(key_list[12], 1), 0, PAIRS_DEV - 1).astype(jnp.int32)
    coupj_target = with_ends(jax.random.randint(key_list[13], (COUPJ,), 0, PAIRS_DEV), jax.random.fold_in(key_list[13], 1), 0, PAIRS_DEV - 1).astype(jnp.int32)
    coupj_fock = jnp.clip(jax.random.uniform(key_list[14], (COUPJ,), jnp.float32, -0.5, 0.5) * shard_levels(key_list[14], (COUPJ,), ((0, 128),), -0.4, 0.0), -0.5, 0.5)
    coupj_correlation = draw_coupj_correlation(jax.random.fold_in(key_list[16], 71), 0)
    return {"factors": factors, "pno_vecs": pno_vecs, "pair_occ": pair_occ, "pno_count": pno_count, "pno_energy": pno_energy, "occ_energy": occ_energy, "coupi_peer": coupi_peer, "coupi_slot": coupi_slot, "coupi_target": coupi_target, "coupi_fock": coupi_fock, "coupi_correlation": coupi_correlation, "coupj_peer": coupj_peer, "coupj_slot": coupj_slot, "coupj_target": coupj_target, "coupj_fock": coupj_fock, "coupj_correlation": coupj_correlation}


def coupling_sum(amplitude, correlation, fock, source, target):
    highest = lax.Precision.HIGHEST

    def single(inputs):
        matrix, weight, source_index = inputs
        half_done = jnp.dot(matrix, amplitude[source_index], precision=highest)
        return weight * jnp.dot(half_done, matrix.T, precision=highest)

    coupling_terms = lax.map(single, (correlation, fock, source))
    return jnp.zeros_like(amplitude).at[target].add(coupling_terms)


def reference(factors, pno_vecs, pair_occ, pno_count, pno_energy, occ_energy, coupi_peer, coupi_slot, coupi_target, coupi_fock, coupi_correlation, coupj_peer, coupj_slot, coupj_target, coupj_fock, coupj_correlation):
    highest = lax.Precision.HIGHEST
    pair_count = pair_occ.shape[0]
    occ_first = pair_occ[:, 0]
    occ_second = pair_occ[:, 1]
    groups = pair_count // 8

    def integrals(inputs):
        rows_first, rows_second, vectors = inputs
        left_half = jnp.einsum('gqv,gva->gqa', factors[rows_first], vectors, precision=highest)
        right_half = jnp.einsum('gqv,gva->gqa', factors[rows_second], vectors, precision=highest)
        return jnp.einsum('gqa,gqb->gab', left_half, right_half, precision=highest)

    integral = lax.map(integrals, (occ_first.reshape(groups, 8), occ_second.reshape(groups, 8), pno_vecs.reshape(groups, 8, NVIR, NPNO)))
    integral = integral.reshape(pair_count, NPNO, NPNO)
    live_pno = (jnp.arange(NPNO)[None, :] < pno_count[:, None]).astype(jnp.float32)
    window = live_pno[:, :, None] * live_pno[:, None, :]
    integral = integral * window
    denominator = pno_energy[:, :, None] + pno_energy[:, None, :] - (occ_energy[occ_first] + occ_energy[occ_second])[:, None, None]
    device_i = (jnp.arange(coupi_peer.shape[0]) // COUPI_DEV).astype(jnp.int32)
    target_i = device_i * PAIRS_DEV + coupi_target
    source_i = (coupi_peer[:, 0] * N_OCCJ + device_i % N_OCCJ) * PAIRS_DEV + coupi_slot
    device_j = (jnp.arange(coupj_peer.shape[0]) // COUPJ_DEV).astype(jnp.int32)
    target_j = device_j * PAIRS_DEV + coupj_target
    source_j = ((device_j // N_OCCJ) * N_OCCJ + coupj_peer[:, 0]) * PAIRS_DEV + coupj_slot
    amplitude = -integral / denominator
    residual = jnp.zeros_like(amplitude)
    for iteration in range(ITERS):
        coupled_i = coupling_sum(amplitude, coupi_correlation, coupi_fock, source_i, target_i)
        coupled_j = coupling_sum(amplitude, coupj_correlation, coupj_fock, source_j, target_j)
        residual = window * (integral + denominator * amplitude - coupled_i - coupled_j)
        amplitude = amplitude - residual / denominator
    return amplitude, residual
```

```python
import functools

import jax
import jax.numpy as jnp
from jax import lax
from jax.experimental import pallas as pl
from jax.experimental.pallas import tpu as pltpu
from jax.sharding import PartitionSpec as P

MESH = pl.DeviceIdType.MESH
f32 = jnp.float32
bf16 = jnp.bfloat16
NI, NJ = 8, 16
CAPI, CAPJ = 8, 4
NP = 64
NC = 64
WAVES = 2
ROWS = 512 // WAVES
VMEM_ALL = 60 * 2**20

OFF_I = [(2, 0), (2, 1), (1, 0), (3, 0), (1, 1), (3, 1), (0, 1)]
OFF_J = sorted(
    [(a, b) for a in range(4) for b in range(4) if (a, b) != (0, 0)],
    key=lambda t: -(min(t[0], 4 - t[0]) + min(t[1], 4 - t[1])),
)


def split(x):
    hi = x.astype(bf16)
    return hi, (x - hi.astype(f32)).astype(bf16)


def dot(a, b):
    return jnp.dot(a, b, preferred_element_type=f32)


def dot_t(a, b):
    return lax.dot_general(a, b, (((1,), (1,)), ((), ())), preferred_element_type=f32)


def peer_i(u, off):
    return ((u // 2 + off[0]) % 4) * 2 + (u % 2 + off[1]) % 2


def peer_j(v, off):
    return ((v // 4 + off[0]) % 4) * 4 + (v % 4 + off[1]) % 4


def back(off, sizes):
    return tuple((n - o) % n for o, n in zip(off, sizes))


def greet(u, v):
    barrier = pltpu.get_barrier_semaphore()
    for off in OFF_I:
        pl.semaphore_signal(barrier, inc=1, device_id={"occi": peer_i(u, off)}, device_id_type=MESH)
    for off in OFF_J:
        pl.semaphore_signal(barrier, inc=1, device_id={"occj": peer_j(v, off)}, device_id_type=MESH)
    pl.semaphore_wait(barrier, len(OFF_I) + len(OFF_J))


def tables_kernel(pi, si, ti, pj, sj, tj, ri, rj, src, order, same, last, ci, cj, cnt):
    ri[...] = jnp.zeros_like(ri)
    rj[...] = jnp.zeros_like(rj)

    def zero(k, c):
        cnt[k] = 0
        return c

    lax.fori_loop(0, NP + 1, zero, 0)
    for k in range(NI):
        ci[k] = 0
    for k in range(NJ):
        cj[k] = 0

    def place_i(c, carry):
        p = pi[c]
        k = ci[p]
        ci[p] = k + 1
        ri[p, pl.ds(k, 1), :] = jnp.full((1, 128), si[c], jnp.int32)
        src[c] = p * CAPI + k
        t = ti[c]
        cnt[t + 1] = cnt[t + 1] + 1
        return carry

    def place_j(c, carry):
        p = pj[c]
        k = cj[p]
        cj[p] = k + 1
        rj[p, pl.ds(k, 1), :] = jnp.full((1, 128), sj[c], jnp.int32)
        src[32 + c] = NI * CAPI + p * CAPJ + k
        t = tj[c]
        cnt[t + 1] = cnt[t + 1] + 1
        return carry

    lax.fori_loop(0, 32, place_i, 0)
    lax.fori_loop(0, 32, place_j, 0)

    def prefix(p, carry):
        n = cnt[p + 1]
        cnt[p + 1] = carry + n
        last[p] = jnp.where(n > 0, carry + n - 1, NC)
        return carry + n

    lax.fori_loop(0, NP, prefix, 0)

    def sort(t, c):
        s = cnt[t]
        cnt[t] = s + 1
        order[s] = c
        same[s] = jnp.where(last[t] == s, 1, 0)

    def sort_i(c, carry):
        sort(ti[c], c)
        return carry

    def sort_j(c, carry):
        sort(tj[c], c + 32)
        return carry

    lax.fori_loop(0, 32, sort_i, 0)
    lax.fori_loop(0, 32, sort_j, 0)

    def shift(k, carry):
        s = NC - 1 - k
        before = same[jnp.maximum(s - 1, 0)]
        same[s] = jnp.where(s == 0, 0, 1 - before)
        return carry

    lax.fori_loop(0, NC, shift, 0)


def tables(pi, si, ti, pj, sj, tj):
    smem = pl.BlockSpec(memory_space=pltpu.SMEM)
    vmem = pl.BlockSpec(memory_space=pltpu.VMEM)
    i32 = jnp.int32
    return pl.pallas_call(
        tables_kernel,
        out_shape=(
            jax.ShapeDtypeStruct((NI, 8, 128), i32),
            jax.ShapeDtypeStruct((NJ, 8, 128), i32),
            jax.ShapeDtypeStruct((NC,), i32),
            jax.ShapeDtypeStruct((NC,), i32),
            jax.ShapeDtypeStruct((NC,), i32),
            jax.ShapeDtypeStruct((NP,), i32),
        ),
        in_specs=[smem] * 6,
        out_specs=(vmem, vmem, smem, smem, smem, smem),
        scratch_shapes=[pltpu.SMEM((NI,), i32), pltpu.SMEM((NJ,), i32), pltpu.SMEM((NP + 1,), i32)],
    )(pi, si, ti, pj, sj, tj)


def gather_kernel(fac, ri, rj, fi, fj, qi, qj, own_sem, tab_sem, rs, ss, crs, css):
    u = lax.axis_index("occi")
    v = lax.axis_index("occj")
    x, z = v % 4, v // 4
    y, core = u // 2, u % 2

    def vid(zz, xx):
        return ((z + zz) % 4) * 4 + (x + xx) % 4

    def uid(yy, cc):
        return ((y + yy) % 4) * 2 + (core + cc) % 2

    greet(u, v)
    pending = []

    own = [
        pltpu.make_async_copy(fac.at[0], fi.at[v], own_sem.at[0]),
        pltpu.make_async_copy(fac.at[0], fj.at[u], own_sem.at[1]),
        pltpu.make_async_copy(ri.at[u], qi.at[u], own_sem.at[2]),
        pltpu.make_async_copy(rj.at[v], qj.at[v], own_sem.at[3]),
    ]
    for c in own:
        c.start()
    waits = []
    for k, off in enumerate(OFF_I):
        to, frm = peer_i(u, off), peer_i(u, back(off, (4, 2)))
        c = pltpu.make_async_remote_copy(ri.at[to], qi.at[u], tab_sem.at[0, k], tab_sem.at[1, k], {"occi": to}, MESH)
        c.start()
        pending.append(c)
        waits.append(pltpu.make_async_remote_copy(ri.at[frm], qi.at[frm], tab_sem.at[0, k], tab_sem.at[1, k], {"occi": to}, MESH))
    for k, off in enumerate(OFF_J):
        to, frm = peer_j(v, off), peer_j(v, back(off, (4, 4)))
        c = pltpu.make_async_remote_copy(rj.at[to], qj.at[v], tab_sem.at[0, 7 + k], tab_sem.at[1, 7 + k], {"occj": to}, MESH)
        c.start()
        pending.append(c)
        waits.append(pltpu.make_async_remote_copy(rj.at[frm], qj.at[frm], tab_sem.at[0, 7 + k], tab_sem.at[1, 7 + k], {"occj": to}, MESH))

    def send(src, buf, slot, q, n, sem, dev):
        at = buf.at[slot, pl.ds(q, n)]
        c = pltpu.make_async_remote_copy(at if src is None else src.at[0, pl.ds(q, n)], at, sem[0], sem[1], dev, MESH)
        c.start()
        pending.append(c)

    def got(buf, slot, q, n, sem, dev):
        at = buf.at[slot, pl.ds(q, n)]
        pltpu.make_async_remote_copy(at, at, sem[0], sem[1], dev, MESH).wait_recv()

    def wave(w):
        h = ROWS // 2
        s = h // 2

        def sem(half, k):
            return ss.at[w, half, k], rs.at[w, half, k]

        halves = []
        for half in (0, 1):
            q = w * ROWS + half * h
            if half == 0:
                first = lambda d: {"occj": vid(0, d)}
                second = lambda d: {"occj": vid(d, 0)}
                slot = lambda a, b: vid(b, a)
            else:
                first = lambda d: {"occj": vid(d, 0)}
                second = lambda d: {"occj": vid(0, d)}
                slot = lambda a, b: vid(a, b)
            halves.append((half, q, first, second, slot))

        def second_send(half, q, second, slot, a, base, src=None):
            send(src, fi, slot(a, 0), q, h, sem(half, base), second(1))
            send(src, fi, slot(a, 0), q, h, sem(half, base + 1), second(3))

        def second_forward(half, q, second, slot, a, base):
            got(fi, slot(a, 3), q, h, sem(half, base), second(1))
            send(None, fi, slot(a, 3), q, s, sem(half, base + 2), second(1))
            got(fi, slot(a, 1), q, h, sem(half, base + 1), second(1))
            send(None, fi, slot(a, 1), q + s, s, sem(half, base + 3), second(3))

        def s0():
            for half, q, first, second, slot in halves:
                send(fac, fi, v, q, h, sem(half, 0), first(1))
                send(fac, fi, v, q, h, sem(half, 1), first(3))
            for half, q, first, second, slot in halves:
                second_send(half, q, second, slot, 0, 4, fac)
            q = w * ROWS
            send(fac, fj, u, q, ROWS, (css.at[w, 0], crs.at[w, 0]), {"occi": uid(1, 0)})
            send(fac, fj, u, q, ROWS, (css.at[w, 1], crs.at[w, 1]), {"occi": uid(3, 0)})
            send(fac, fj, u, q, ROWS, (css.at[w, 4], crs.at[w, 4]), {"occi": uid(0, 1)})

        def s1():
            for half, q, first, second, slot in halves:
                got(fi, slot(3, 0), q, h, sem(half, 0), first(1))
                send(None, fi, slot(3, 0), q, s, sem(half, 2), first(1))
                got(fi, slot(1, 0), q, h, sem(half, 1), first(1))
                send(None, fi, slot(1, 0), q + s, s, sem(half, 3), first(3))
            for half, q, first, second, slot in halves:
                second_send(half, q, second, slot, 3, 8)
                second_send(half, q, second, slot, 1, 12)

        def s2():
            for half, q, first, second, slot in halves:
                second_forward(half, q, second, slot, 0, 4)
            q, n = w * ROWS, ROWS // 2
            got(fj, uid(3, 0), q, ROWS, (css.at[w, 0], crs.at[w, 0]), {"occi": uid(1, 0)})
            send(None, fj, uid(3, 0), q, n, (css.at[w, 2], crs.at[w, 2]), {"occi": uid(1, 0)})
            send(None, fj, uid(3, 0), q, ROWS, (css.at[w, 5], crs.at[w, 5]), {"occi": uid(0, 1)})
            got(fj, uid(1, 0), q, ROWS, (css.at[w, 1], crs.at[w, 1]), {"occi": uid(1, 0)})
            send(None, fj, uid(1, 0), q + n, n, (css.at[w, 3], crs.at[w, 3]), {"occi": uid(3, 0)})
            send(None, fj, uid(1, 0), q, ROWS, (css.at[w, 6], crs.at[w, 6]), {"occi": uid(0, 1)})

        def s3():
            for half, q, first, second, slot in halves:
                got(fi, slot(2, 0), q, s, sem(half, 2), first(1))
                got(fi, slot(2, 0), q + s, s, sem(half, 3), first(1))
                second_send(half, q, second, slot, 2, 16)

        def s4():
            for half, q, first, second, slot in halves:
                second_forward(half, q, second, slot, 3, 8)
                second_forward(half, q, second, slot, 1, 12)
            q, n = w * ROWS, ROWS // 2
            got(fj, uid(2, 0), q, n, (css.at[w, 2], crs.at[w, 2]), {"occi": uid(1, 0)})
            got(fj, uid(2, 0), q + n, n, (css.at[w, 3], crs.at[w, 3]), {"occi": uid(1, 0)})
            send(None, fj, uid(2, 0), q, ROWS, (css.at[w, 7], crs.at[w, 7]), {"occi": uid(0, 1)})

        def s5():
            for half, q, first, second, slot in halves:
                second_forward(half, q, second, slot, 2, 16)

        def s6():
            for half, q, first, second, slot in halves:
                for a, base in ((0, 4), (3, 8), (1, 12), (2, 16)):
                    got(fi, slot(a, 2), q, s, sem(half, base + 2), second(1))
                    got(fi, slot(a, 2), q + s, s, sem(half, base + 3), second(1))
            q = w * ROWS
            for k, yy in ((4, 0), (5, 3), (6, 1), (7, 2)):
                got(fj, uid(yy, 1), q, ROWS, (css.at[w, k], crs.at[w, k]), {"occi": uid(0, 1)})

        return s0, s1, s2, s3, s4, s5, s6

    a, b = wave(0), wave(1)
    for step in (a[0], a[1], b[0], a[2], a[3], b[1], a[4], b[2], a[5], b[3], b[4], a[6], b[5], b[6]):
        step()
    for c in waits:
        c.wait_recv()
    for c in pending:
        c.wait_send()
    for c in own:
        c.wait()


def gather(factors, ri, rj):
    anyw = pl.BlockSpec(memory_space=pl.ANY)
    i32 = jnp.int32
    dma = pltpu.SemaphoreType.DMA
    return pl.pallas_call(
        gather_kernel,
        out_shape=(
            jax.ShapeDtypeStruct((NJ, 512, 256), f32),
            jax.ShapeDtypeStruct((NI, 512, 256), f32),
            jax.ShapeDtypeStruct((NI, 8, 128), i32),
            jax.ShapeDtypeStruct((NJ, 8, 128), i32),
        ),
        in_specs=[anyw] * 3,
        out_specs=(anyw,) * 4,
        scratch_shapes=[
            dma((4,)),
            dma((2, 22)),
            dma((WAVES, 2, 20)),
            dma((WAVES, 2, 20)),
            dma((WAVES, 8)),
            dma((WAVES, 8)),
        ],
        compiler_params=pltpu.CompilerParams(collective_id=0, has_side_effects=True, vmem_limit_bytes=VMEM_ALL),
    )(factors, ri, rj)


GROUP = 4


def integral_kernel(occ, cnt, eo, fi, fj, v_ref, en, amp, inv, th, tl, jh, jl):
    step = pl.program_id(0)
    u = lax.axis_index("occi")

    @pl.when(step == 0)
    def _():
        def bi(k, c):
            h, l = split(jnp.transpose(fi[k]))
            th[k] = h
            tl[k] = l
            return c

        def bj(k, c):
            h, l = split(fj[k])
            jh[k] = h
            jl[k] = l
            return c

        lax.fori_loop(0, NJ, bi, 0)
        lax.fori_loop(0, NI, bj, 0)

    rows = lax.broadcasted_iota(jnp.int32, (128, 128), 0)
    cols = lax.broadcasted_iota(jnp.int32, (128, 128), 1)

    for g in range(GROUP):
        p = step * GROUP + g
        oi, oj = occ[0, p], occ[1, p]
        i, j = oi - u * NJ, oj // NJ
        vec = v_ref[g]
        vh, vl = split(vec)
        vth, vtl = split(jnp.transpose(vec))
        t2 = dot(jnp.concatenate([vth, vtl], axis=0), th[i])
        lt = t2[:128] + t2[128:] + dot(vth, tl[i])
        r2 = dot(jh[j], jnp.concatenate([vh, vl], axis=1))
        r = r2[:, :128] + r2[:, 128:] + dot(jl[j], vh)
        lh, ll = split(lt)
        rh, rl = split(r)
        o = dot(jnp.concatenate([lh, ll], axis=0), jnp.concatenate([rh, rl], axis=1))
        o = (o[:128, :128] + o[:128, 128:]) + o[128:, :128]
        across = jnp.broadcast_to(en[pl.ds(g, 1), :] if False else en[0, pl.ds(g, 1), :], (128, 128))
        den = jnp.transpose(across) + across - (eo[oi] + eo[oj])
        n = cnt[p]
        m = jnp.where((rows < n) & (cols < n), 1.0 / den, 0.0)
        inv[g] = m
        amp[g] = -o * m


def integrals(occ, cnt, eo, fi, fj, vecs, en):
    smem = pl.BlockSpec(memory_space=pltpu.SMEM)
    vmem = pl.BlockSpec(memory_space=pltpu.VMEM)
    block = pl.BlockSpec((GROUP, 128, 128), lambda s: (s, 0, 0))
    return pl.pallas_call(
        integral_kernel,
        grid=(NP // GROUP,),
        out_shape=(jax.ShapeDtypeStruct((NP, 128, 128), f32),) * 2,
        in_specs=[
            smem,
            smem,
            smem,
            vmem,
            vmem,
            pl.BlockSpec((GROUP, 256, 128), lambda s: (s, 0, 0)),
            pl.BlockSpec((1, GROUP, 128), lambda s: (s, 0, 0)),
        ],
        out_specs=(block, block),
        scratch_shapes=[pltpu.VMEM((NJ, 256, 512), bf16)] * 2 + [pltpu.VMEM((NI, 512, 256), bf16)] * 2,
        compiler_params=pltpu.CompilerParams(vmem_limit_bytes=VMEM_ALL),
    )(occ, cnt, eo, fi, fj, vecs, en.reshape(NP // GROUP, GROUP, 128))


UNROLL = 4
SEND = 7 * CAPI + 15 * CAPJ


def iterate_kernel(
    qi, qj, src, order, same, last, fock, cnt, amp0, inv0, ci, cj, amp_out, res_out,
    amp, inv, corr, delta, term, snd, rcv0, rcv1, ls, ss, rs,
):
    u = lax.axis_index("occi")
    v = lax.axis_index("occj")
    arrived = (rcv0, rcv1)
    loads = [
        pltpu.make_async_copy(amp0, amp, ls.at[0]),
        pltpu.make_async_copy(inv0, inv, ls.at[1]),
        pltpu.make_async_copy(ci, corr.at[pl.ds(0, 32)], ls.at[2]),
        pltpu.make_async_copy(cj, corr.at[pl.ds(32, 32)], ls.at[3]),
    ]
    for c in loads:
        c.start()
    greet(u, v)
    term[NC] = jnp.zeros((128, 128), f32)

    def exchange(it, x):
        copies, waits = [], []
        at_i, at_j = 0, 7 * CAPI
        jobs = []
        for k in range(15):
            if k < 7:
                jobs.append((0, k))
            jobs.append((1, k))
        for axis, k in jobs:
            if axis == 0:
                off, cap, q, name, base = OFF_I[k], CAPI, qi, "occi", k * CAPI
                to, frm, mine = peer_i(u, off), peer_i(u, back(off, (4, 2))), u * CAPI
                came, sem = frm * CAPI, k
            else:
                off, cap, q, name, base = OFF_J[k], CAPJ, qj, "occj", 7 * CAPI + k * CAPJ
                to, frm, mine = peer_j(v, off), peer_j(v, back(off, (4, 4))), NI * CAPI + v * CAPJ
                came, sem = NI * CAPI + frm * CAPJ, 7 + k
            for s in range(cap):
                snd[base + s] = x[q[to, s]]
            c = pltpu.make_async_remote_copy(
                snd.at[pl.ds(base, cap)], arrived[it].at[pl.ds(mine, cap)], ss.at[it, sem], rs.at[it, sem], {name: to}, MESH
            )
            c.start()
            copies.append(c)
            waits.append(
                pltpu.make_async_remote_copy(
                    snd.at[pl.ds(base, cap)], arrived[it].at[pl.ds(came, cap)], ss.at[it, sem], rs.at[it, sem], {name: to}, MESH
                )
            )
        for s in range(CAPI):
            arrived[it][u * CAPI + s] = x[qi[u, s]]
        for s in range(CAPJ):
            arrived[it][NI * CAPI + v * CAPJ + s] = x[qj[v, s]]
        return copies, waits

    def couple(it):
        def body(b, run):
            for k in range(UNROLL):
                s = b * UNROLL + k
                c = order[s]
                m = corr[c]
                mh, ml = split(m)
                xh, xl = split(arrived[it][src[c]])
                xx = jnp.concatenate([xh, xl], axis=1)
                h = dot(jnp.concatenate([mh, ml], axis=1), jnp.concatenate([xx, xx], axis=0))
                hh, hl = split(h[:, :128] + h[:, 128:])
                m4 = jnp.concatenate([jnp.concatenate([mh, mh], axis=1), jnp.concatenate([ml, ml], axis=1)], axis=0)
                t = dot_t(jnp.concatenate([hh, hl], axis=1), m4)
                t = (t[:, :128] + t[:, 128:]) * fock[c]
                run = jnp.where(same[s] > 0, run, 0.0) + t
                term[s] = run
            return run

        lax.fori_loop(0, NC // UNROLL, body, jnp.zeros((128, 128), f32))

    for c in loads:
        c.wait()
    copies, waits = exchange(0, amp)
    for c in waits:
        c.wait_recv()
    for c in copies:
        c.wait_send()
    couple(0)

    def first(p, carry):
        delta[p] = term[last[p]] * inv[p]
        return carry

    lax.fori_loop(0, NP, first, 0)
    copies, waits = exchange(1, delta)
    for c in waits:
        c.wait_recv()
    for c in copies:
        c.wait_send()
    couple(1)
    rows = lax.broadcasted_iota(jnp.int32, (128, 128), 0)
    cols = lax.broadcasted_iota(jnp.int32, (128, 128), 1)

    def second(p, carry):
        s = term[last[p]]
        n = cnt[p]
        amp[p] = amp[p] + delta[p] + s * inv[p]
        inv[p] = jnp.where((rows < n) & (cols < n), -s, 0.0)
        return carry

    lax.fori_loop(0, NP, second, 0)
    outs = [pltpu.make_async_copy(amp, amp_out, ls.at[0]), pltpu.make_async_copy(inv, res_out, ls.at[1])]
    for c in outs:
        c.start()
    for c in outs:
        c.wait()


def iterate(qi, qj, src, order, same, last, fock, cnt, amp, inv, ci, cj):
    smem = pl.BlockSpec(memory_space=pltpu.SMEM)
    anyw = pl.BlockSpec(memory_space=pl.ANY)
    dma = pltpu.SemaphoreType.DMA
    mats = lambda n: pltpu.VMEM((n, 128, 128), f32)
    return pl.pallas_call(
        iterate_kernel,
        out_shape=(jax.ShapeDtypeStruct((NP, 128, 128), f32),) * 2,
        in_specs=[smem] * 8 + [anyw] * 4,
        out_specs=(anyw, anyw),
        scratch_shapes=[
            mats(NP),
            mats(NP),
            mats(NC),
            mats(NP),
            mats(NC + 1),
            mats(SEND),
            mats(NI * CAPI + NJ * CAPJ),
            mats(NI * CAPI + NJ * CAPJ),
            dma((4,)),
            dma((2, 22)),
            dma((2, 22)),
        ],
        compiler_params=pltpu.CompilerParams(collective_id=1, has_side_effects=True, vmem_limit_bytes=VMEM_ALL),
    )(qi, qj, src, order, same, last, fock, cnt, amp, inv, ci, cj)


def local(
    factors, pno_vecs, pair_occ, pno_count, pno_energy, occ_energy,
    coupi_peer, coupi_slot, coupi_target, coupi_fock, coupi_correlation,
    coupj_peer, coupj_slot, coupj_target, coupj_fock, coupj_correlation,
):
    ri, rj, src, order, same, last = tables(
        coupi_peer[:, 0], coupi_slot, coupi_target, coupj_peer[:, 0], coupj_slot, coupj_target
    )
    fi, fj, qi, qj = gather(factors, ri, rj)
    amp, inv = integrals(pair_occ.T, pno_count, occ_energy, fi, fj, pno_vecs, pno_energy)
    fock = jnp.concatenate([coupi_fock, coupj_fock])
    return iterate(
        qi[:, :, 0], qj[:, :CAPJ, 0], src, order, same, last, fock, pno_count, amp, inv, coupi_correlation, coupj_correlation
    )


def solution(mesh):
    both = ("occi", "occj")
    three, two, one = P(both, None, None), P(both, None), P(both)
    placed = (
        three, three, two, one, two, P(),
        two, one, one, one, three,
        two, one, one, one, three,
    )
    return jax.shard_map(local, mesh=mesh, in_specs=placed, out_specs=(three, three), check_vma=False)
```

```python
import functools

import jax
import jax.numpy as jnp
from jax import lax
from jax.experimental import pallas as pl
from jax.experimental.pallas import tpu as pltpu
from jax.sharding import PartitionSpec as P

MESH = pl.DeviceIdType.MESH
f32 = jnp.float32
bf16 = jnp.bfloat16
NI, NJ = 8, 16
CAPI, CAPJ = 8, 4
NP = 64
NC = 64
WAVES = 2
ROWS = 512 // WAVES
VMEM_ALL = 60 * 2**20
GROUP = 4

OFF_I = [(2, 0), (2, 1), (1, 0), (3, 0), (1, 1), (3, 1), (0, 1)]
OFF_J = sorted(
    [(a, b) for a in range(4) for b in range(4) if (a, b) != (0, 0)],
    key=lambda t: -(min(t[0], 4 - t[0]) + min(t[1], 4 - t[1])),
)


def split(x):
    hi = x.astype(bf16)
    return hi, (x - hi.astype(f32)).astype(bf16)


def dot(a, b):
    return jnp.dot(a, b, preferred_element_type=f32)


def dot_t(a, b):
    return lax.dot_general(a, b, (((1,), (1,)), ((), ())), preferred_element_type=f32)


def peer_i(u, off):
    return ((u // 2 + off[0]) % 4) * 2 + (u % 2 + off[1]) % 2


def peer_j(v, off):
    return ((v // 4 + off[0]) % 4) * 4 + (v % 4 + off[1]) % 4


def back(off, sizes):
    return tuple((n - o) % n for o, n in zip(off, sizes))


def greet(u, v):
    barrier = pltpu.get_barrier_semaphore()
    for off in OFF_I:
        pl.semaphore_signal(barrier, inc=1, device_id={"occi": peer_i(u, off)}, device_id_type=MESH)
    for off in OFF_J:
        pl.semaphore_signal(barrier, inc=1, device_id={"occj": peer_j(v, off)}, device_id_type=MESH)
    pl.semaphore_wait(barrier, len(OFF_I) + len(OFF_J))


def tables(tab, ri, rj, plan, weight):
    lane = lax.broadcasted_iota(jnp.int32, (NC, 128), 1)
    sub = lax.broadcasted_iota(jnp.int32, (NC, 128), 0)

    def across(r):
        return jnp.broadcast_to(tab[pl.ds(r, 1), :], (128, 128))

    def down(r):
        return jnp.transpose(across(r))[:NC]

    def count(mask, axis):
        return jnp.sum(jnp.where(mask, 1.0, 0.0), axis=axis, keepdims=True)

    def pick(mask, value):
        return jnp.sum(jnp.where(mask, value, 0.0), axis=0, keepdims=True)

    peer, slot, target, fock = down(0), down(1), down(2), down(3)
    rank = count((across(0)[:NC] == peer) & (lane < sub), 1)
    at = rank.astype(jnp.int32)
    for p in range(NI):
        ri[p] = pick((peer == p) & (at == lane), slot).astype(jnp.int32)
    for p in range(NJ):
        rj[p] = pick((peer == NI + p) & (at == lane), slot).astype(jnp.int32)
    arrival = jnp.where(peer < NI, peer * CAPI, NI * CAPI + (peer - NI) * CAPJ) + rank
    row_t = across(2)[:NC]
    equal = row_t == target
    place = count((row_t < target) | (equal & (lane < sub)), 1).astype(jnp.int32)
    goes_on = jnp.minimum(count(equal & (lane < sub), 1), 1.0)
    here = place == lane
    plan[pl.ds(0, 1), :] = pick(here, sub.astype(f32)).astype(jnp.int32)
    plan[pl.ds(1, 1), :] = pick(here, arrival).astype(jnp.int32)
    plan[pl.ds(2, 1), :] = pick(here, goes_on).astype(jnp.int32)
    lane_f = lane.astype(f32)
    upto = count(target <= lane_f, 0)
    plan[pl.ds(3, 1), :] = jnp.where(count(target == lane_f, 0) > 0.5, upto - 1.0, float(NC)).astype(jnp.int32)
    weight[...] = pick(here, fock)


def integral_kernel(
    occ, cnt, eo, tab, en, fac, vecs, amp, qi, qj, plan, weight,
    fi0, fi1, fj0, fj1, th, tl, jh, jl, vec, acc, ri, rj, own_sem, tab_sem, rs, ss, crs, css, out_sem,
):
    u = lax.axis_index("occi")
    v = lax.axis_index("occj")
    x, z = v % 4, v // 4
    y, core = u // 2, u % 2
    fi, fj = (fi0, fi1), (fj0, fj1)

    def vid(zz, xx):
        return ((z + zz) % 4) * 4 + (x + xx) % 4

    def uid(yy, cc):
        return ((y + yy) % 4) * 2 + (core + cc) % 2

    own = [pltpu.make_async_copy(vecs, vec, own_sem.at[0])]
    for w in range(WAVES):
        at = fac.at[0, pl.ds(w * ROWS, ROWS)]
        own.append(pltpu.make_async_copy(at, fi[w].at[v], own_sem.at[1 + 2 * w]))
        own.append(pltpu.make_async_copy(at, fj[w].at[u], own_sem.at[2 + 2 * w]))
    greet(u, v)
    for c in own:
        c.start()
    pending = []

    def send(w, from_fac, buf, slot, q, n, sem, dev):
        at = buf[w].at[slot, pl.ds(q, n)]
        src = fac.at[0, pl.ds(w * ROWS + q, n)] if from_fac else at
        c = pltpu.make_async_remote_copy(src, at, sem[0], sem[1], dev, MESH)
        c.start()
        pending.append(c)

    def got(w, buf, slot, q, n, sem, dev):
        at = buf[w].at[slot, pl.ds(q, n)]
        pltpu.make_async_remote_copy(at, at, sem[0], sem[1], dev, MESH).wait_recv()

    def wave(w):
        h = ROWS // 2
        s = h // 2

        def sem(half, k):
            return ss.at[w, half, k], rs.at[w, half, k]

        def csem(k):
            return css.at[w, k], crs.at[w, k]

        halves = []
        for half in (0, 1):
            if half == 0:
                first = lambda d: {"occj": vid(0, d)}
                second = lambda d: {"occj": vid(d, 0)}
                slot = lambda a, b: vid(b, a)
            else:
                first = lambda d: {"occj": vid(d, 0)}
                second = lambda d: {"occj": vid(0, d)}
                slot = lambda a, b: vid(a, b)
            halves.append((half, half * h, first, second, slot))

        def second_send(half, q, second, slot, a, base, mine=False):
            send(w, mine, fi, slot(a, 0), q, h, sem(half, base), second(1))
            send(w, mine, fi, slot(a, 0), q, h, sem(half, base + 1), second(3))

        def second_forward(half, q, second, slot, a, base):
            got(w, fi, slot(a, 3), q, h, sem(half, base), second(1))
            send(w, False, fi, slot(a, 3), q, s, sem(half, base + 2), second(1))
            got(w, fi, slot(a, 1), q, h, sem(half, base + 1), second(1))
            send(w, False, fi, slot(a, 1), q + s, s, sem(half, base + 3), second(3))

        def s0():
            for half, q, first, second, slot in halves:
                send(w, True, fi, v, q, h, sem(half, 0), first(1))
                send(w, True, fi, v, q, h, sem(half, 1), first(3))
            for half, q, first, second, slot in halves:
                second_send(half, q, second, slot, 0, 4, True)
            send(w, True, fj, u, 0, ROWS, csem(0), {"occi": uid(1, 0)})
            send(w, True, fj, u, 0, ROWS, csem(1), {"occi": uid(3, 0)})
            send(w, True, fj, u, 0, ROWS, csem(4), {"occi": uid(0, 1)})

        def s1():
            for half, q, first, second, slot in halves:
                got(w, fi, slot(3, 0), q, h, sem(half, 0), first(1))
                send(w, False, fi, slot(3, 0), q, s, sem(half, 2), first(1))
                got(w, fi, slot(1, 0), q, h, sem(half, 1), first(1))
                send(w, False, fi, slot(1, 0), q + s, s, sem(half, 3), first(3))
            for half, q, first, second, slot in halves:
                second_send(half, q, second, slot, 3, 8)
                second_send(half, q, second, slot, 1, 12)

        def s2():
            for half, q, first, second, slot in halves:
                second_forward(half, q, second, slot, 0, 4)
            n = ROWS // 2
            got(w, fj, uid(3, 0), 0, ROWS, csem(0), {"occi": uid(1, 0)})
            send(w, False, fj, uid(3, 0), 0, n, csem(2), {"occi": uid(1, 0)})
            send(w, False, fj, uid(3, 0), 0, ROWS, csem(5), {"occi": uid(0, 1)})
            got(w, fj, uid(1, 0), 0, ROWS, csem(1), {"occi": uid(1, 0)})
            send(w, False, fj, uid(1, 0), n, n, csem(3), {"occi": uid(3, 0)})
            send(w, False, fj, uid(1, 0), 0, ROWS, csem(6), {"occi": uid(0, 1)})

        def s3():
            for half, q, first, second, slot in halves:
                got(w, fi, slot(2, 0), q, s, sem(half, 2), first(1))
                got(w, fi, slot(2, 0), q + s, s, sem(half, 3), first(1))
                second_send(half, q, second, slot, 2, 16)

        def s4():
            for half, q, first, second, slot in halves:
                second_forward(half, q, second, slot, 3, 8)
                second_forward(half, q, second, slot, 1, 12)
            n = ROWS // 2
            got(w, fj, uid(2, 0), 0, n, csem(2), {"occi": uid(1, 0)})
            got(w, fj, uid(2, 0), n, n, csem(3), {"occi": uid(1, 0)})
            send(w, False, fj, uid(2, 0), 0, ROWS, csem(7), {"occi": uid(0, 1)})

        def s5():
            for half, q, first, second, slot in halves:
                second_forward(half, q, second, slot, 2, 16)

        def s6():
            for half, q, first, second, slot in halves:
                for a, base in ((0, 4), (3, 8), (1, 12), (2, 16)):
                    got(w, fi, slot(a, 2), q, s, sem(half, base + 2), second(1))
                    got(w, fi, slot(a, 2), q + s, s, sem(half, base + 3), second(1))
            for k, yy in ((4, 0), (5, 3), (6, 1), (7, 2)):
                got(w, fj, uid(yy, 1), 0, ROWS, csem(k), {"occi": uid(0, 1)})

        return s0, s1, s2, s3, s4, s5, s6

    def halve(w):
        def bi(k, c):
            h, l = split(fi[w][k])
            th[k] = h
            tl[k] = l
            return c

        def bj(k, c):
            h, l = split(fj[w][k])
            jh[k] = h
            jl[k] = l
            return c

        lax.fori_loop(0, NJ, bi, 0)
        lax.fori_loop(0, NI, bj, 0)

    rows = lax.broadcasted_iota(jnp.int32, (128, 128), 0)
    cols = lax.broadcasted_iota(jnp.int32, (128, 128), 1)

    def pair(w, p):
        oi, oj = occ[0, p], occ[1, p]
        i, j = lax.rem(oi, NJ), lax.div(oj, NJ)
        o = product(th, tl, jh, jl, i, j, vec[p])
        if w == 0:
            acc[p] = o
            return
        den = denominator(en, p) - (eo[oi] + eo[oj])
        n = cnt[p]
        acc[p] = jnp.where((rows < n) & (cols < n), -(acc[p] + o) / den, 0.0)

    def some(w, lo, hi):
        def body(b, c):
            for g in range(GROUP):
                pair(w, b * GROUP + g)
            return c

        lax.fori_loop(lo // GROUP, hi // GROUP, body, 0)

    a, b = wave(0), wave(1)
    a[0]()
    tables(tab, ri, rj, plan, weight)
    waits = []
    for k, off in enumerate(OFF_I + OFF_J):
        if k < 7:
            to, frm, me, r, q, name = peer_i(u, off), peer_i(u, back(off, (4, 2))), u, ri, qi, "occi"
        else:
            to, frm, me, r, q, name = peer_j(v, off), peer_j(v, back(off, (4, 4))), v, rj, qj, "occj"
        c = pltpu.make_async_remote_copy(r.at[to], q.at[me], tab_sem.at[0, k], tab_sem.at[1, k], {name: to}, MESH)
        c.start()
        pending.append(c)
        waits.append(
            pltpu.make_async_remote_copy(r.at[frm], q.at[frm], tab_sem.at[0, k], tab_sem.at[1, k], {name: to}, MESH)
        )
    qi[u] = ri[u]
    qj[v] = rj[v]
    for step in (a[1], b[0], a[2], a[3], b[1], a[4], b[2], a[5], b[3]):
        step()
    for c in own:
        c.wait()
    a[6]()
    halve(0)
    some(0, 0, 16)
    b[4]()
    some(0, 16, 32)
    b[5]()
    some(0, 32, 64)
    b[6]()
    halve(1)
    outs = []
    for k in range(4):
        some(1, 16 * k, 16 * k + 16)
        part = pl.ds(16 * k, 16)
        c = pltpu.make_async_copy(acc.at[part], amp.at[part], out_sem.at[k])
        c.start()
        outs.append(c)
    for c in waits:
        c.wait_recv()
    for c in pending:
        c.wait_send()
    for c in outs:
        c.wait()


def dot_0(a, b):
    return lax.dot_general(a, b, (((0,), (0,)), ((), ())), preferred_element_type=f32)


def product(th, tl, jh, jl, i, j, vec):
    vth, vtl = split(jnp.transpose(vec))
    v2 = jnp.concatenate([vth, vtl], axis=0)
    a = dot_t(v2, th[i])
    lt = a[:128] + a[128:] + dot_t(vth, tl[i])
    b = dot_t(v2, jh[j])
    rt = b[:128] + b[128:] + dot_t(vth, jl[j])
    lh, ll = split(lt)
    rh, rl = split(rt)
    o = dot_t(jnp.concatenate([lh, ll], axis=0), jnp.concatenate([rh, rl], axis=0))
    return (o[:128, :128] + o[:128, 128:]) + o[128:, :128]


def denominator(en, p):
    across = jnp.broadcast_to(en[pl.ds(p, 1), :], (128, 128))
    return jnp.transpose(across) + across


def integrals(occ, cnt, eo, tab, en, factors, vecs):
    smem = pl.BlockSpec(memory_space=pltpu.SMEM)
    vmem = pl.BlockSpec(memory_space=pltpu.VMEM)
    anyw = pl.BlockSpec(memory_space=pl.ANY)
    i32 = jnp.int32
    dma = pltpu.SemaphoreType.DMA
    return pl.pallas_call(
        integral_kernel,
        out_shape=(
            jax.ShapeDtypeStruct((NP, 128, 128), f32),
            jax.ShapeDtypeStruct((NI, 1, 128), i32),
            jax.ShapeDtypeStruct((NJ, 1, 128), i32),
            jax.ShapeDtypeStruct((8, 128), i32),
            jax.ShapeDtypeStruct((1, 128), f32),
        ),
        in_specs=[smem] * 3 + [vmem] * 2 + [anyw] * 2,
        out_specs=(anyw, vmem, vmem, vmem, vmem),
        scratch_shapes=[
            pltpu.VMEM((NJ, ROWS, 256), f32),
            pltpu.VMEM((NJ, ROWS, 256), f32),
            pltpu.VMEM((NI, ROWS, 256), f32),
            pltpu.VMEM((NI, ROWS, 256), f32),
            pltpu.VMEM((NJ, ROWS, 256), bf16),
            pltpu.VMEM((NJ, ROWS, 256), bf16),
            pltpu.VMEM((NI, ROWS, 256), bf16),
            pltpu.VMEM((NI, ROWS, 256), bf16),
            pltpu.VMEM((NP, 256, 128), f32),
            pltpu.VMEM((NP, 128, 128), f32),
            pltpu.VMEM((NI, 1, 128), i32),
            pltpu.VMEM((NJ, 1, 128), i32),
            dma((5,)),
            dma((2, 22)),
            dma((WAVES, 2, 20)),
            dma((WAVES, 2, 20)),
            dma((WAVES, 8)),
            dma((WAVES, 8)),
            dma((4,)),
        ],
        compiler_params=pltpu.CompilerParams(collective_id=0, has_side_effects=True, vmem_limit_bytes=VMEM_ALL),
    )(occ, cnt, eo, tab, en, factors, vecs)


UNROLL = 4
SLOTS = NI * CAPI + NJ * CAPJ


def couple(plan, weight, corr, arrived, term):
    term[NC] = jnp.zeros((128, 128), f32)

    def body(b, run):
        for k in range(UNROLL):
            s = b * UNROLL + k
            m = corr[plan[0, s]]
            mh, ml = split(m)
            xh, xl = split(arrived[plan[1, s]])
            xx = jnp.concatenate([xh, xl], axis=1)
            h = dot(jnp.concatenate([mh, ml], axis=1), jnp.concatenate([xx, xx], axis=0))
            hh, hl = split(h[:, :128] + h[:, 128:])
            m4 = jnp.concatenate([jnp.concatenate([mh, mh], axis=1), jnp.concatenate([ml, ml], axis=1)], axis=0)
            t = dot_t(jnp.concatenate([hh, hl], axis=1), m4)
            t = (t[:, :128] + t[:, 128:]) * weight[0, s]
            run = jnp.where(plan[2, s] > 0, run, 0.0) + t
            term[s] = run
        return run

    lax.fori_loop(0, NC // UNROLL, body, jnp.zeros((128, 128), f32))


def iterate_kernel(
    qi, qj, plan, weight, occ, cnt, eo, en, amp0, ci, cj, amp_out, res_out,
    amp, inv, corr, delta, term, snd_i, snd_j, mid, rcv0, rcv1, ls, si, ri, sj, rj,
):
    u = lax.axis_index("occi")
    v = lax.axis_index("occj")
    x, z = v % 4, v // 4
    rows = lax.broadcasted_iota(jnp.int32, (128, 128), 0)
    cols = lax.broadcasted_iota(jnp.int32, (128, 128), 1)
    loads = [
        pltpu.make_async_copy(amp0, amp, ls.at[0]),
        pltpu.make_async_copy(ci, corr.at[pl.ds(0, 32)], ls.at[1]),
        pltpu.make_async_copy(cj, corr.at[pl.ds(32, 32)], ls.at[2]),
    ]
    for c in loads:
        c.start()
    greet(u, v)

    def vid(dz, dx):
        return ((z + dz) % 4) * 4 + (x + dx) % 4

    def exchange(it, src, arrived, beside):
        half_rows = CAPJ // 2
        first, rest, sent = {}, [], []

        def fill(half, d):
            for e in range(4):
                if d == 0 and e == 0:
                    continue
                to = vid(e, d) if half == 0 else vid(d, e)
                for s in range(half_rows):
                    snd_j[it, half, d, half_rows * e + s] = src[qj[to, 0, half_rows * half + s]]

        def place(half, d, e):
            frm = vid((4 - e) % 4, (4 - d) % 4) if half == 0 else vid((4 - d) % 4, (4 - e) % 4)
            return arrived.at[pl.ds(NI * CAPI + frm * CAPJ + half_rows * half, half_rows)]

        for d in (2, 1, 3):
            for half in (0, 1):
                fill(half, d)
                to = vid(0, d) if half == 0 else vid(d, 0)
                c = pltpu.make_async_remote_copy(
                    snd_j.at[it, half, d], mid.at[it, half, d], sj.at[it, half, d, 0], rj.at[it, half, d, 0], {"occj": to}, MESH
                )
                c.start()
                first[half, d] = c
                sent.append(c)
        for k, off in enumerate(OFF_I):
            to, frm = peer_i(u, off), peer_i(u, back(off, (4, 2)))
            for s in range(CAPI):
                snd_i[it, k * CAPI + s] = src[qi[to, 0, s]]
            out = snd_i.at[it, pl.ds(k * CAPI, CAPI)]
            c = pltpu.make_async_remote_copy(
                out, arrived.at[pl.ds(u * CAPI, CAPI)], si.at[it, k], ri.at[it, k], {"occi": to}, MESH
            )
            c.start()
            sent.append(c)
            rest.append(
                pltpu.make_async_remote_copy(
                    out, arrived.at[pl.ds(frm * CAPI, CAPI)], si.at[it, k], ri.at[it, k], {"occi": to}, MESH
                )
            )

        def onward(half, d):
            for e in (2, 1, 3):
                to = vid(e, 0) if half == 0 else vid(0, e)
                out = (snd_j if d == 0 else mid).at[it, half, d, pl.ds(half_rows * e, half_rows)]
                start = vid(0, (4 - d) % 4) if half == 0 else vid((4 - d) % 4, 0)
                into = arrived.at[pl.ds(NI * CAPI + start * CAPJ + half_rows * half, half_rows)]
                c = pltpu.make_async_remote_copy(
                    out, into, sj.at[it, half, d, e], rj.at[it, half, d, e], {"occj": to}, MESH
                )
                c.start()
                sent.append(c)
                rest.append(
                    pltpu.make_async_remote_copy(
                        out, place(half, d, e), sj.at[it, half, d, e], rj.at[it, half, d, e], {"occj": to}, MESH
                    )
                )

        for half in (0, 1):
            fill(half, 0)
            onward(half, 0)
        for s in range(CAPI):
            arrived[u * CAPI + s] = src[qi[u, 0, s]]
        for s in range(CAPJ):
            arrived[NI * CAPI + v * CAPJ + s] = src[qj[v, 0, s]]
        beside(0)
        for d in (1, 3, 2):
            for half in (0, 1):
                first[half, d].wait_recv()
                onward(half, d)
            if d == 3:
                beside(1)
        for half in (0, 1):
            for d in (1, 3, 2):
                frm = vid(0, (4 - d) % 4) if half == 0 else vid((4 - d) % 4, 0)
                for s in range(half_rows):
                    arrived[NI * CAPI + frm * CAPJ + half_rows * half + s] = mid[it, half, d, s]
        beside(2)
        for c in rest:
            c.wait_recv()
        for c in sent:
            c.wait_send()

    def inverses(lo, hi):
        def body(p, carry):
            den = denominator(en, p) - (eo[occ[0, p]] + eo[occ[1, p]])
            n = cnt[p]
            inv[p] = jnp.where((rows < n) & (cols < n), 1.0 / den, 0.0)
            return carry

        lax.fori_loop(lo, hi, body, 0)

    def beside0(part):
        if part == 0:
            inverses(0, 16)
        elif part == 1:
            inverses(16, 32)
        else:
            inverses(32, 64)
            for c in loads[1:]:
                c.wait()

    loads[0].wait()
    exchange(0, amp, rcv0, beside0)
    couple(plan, weight, corr, rcv0, term)

    def first(p, carry):
        delta[p] = term[plan[3, p]] * inv[p]
        return carry

    lax.fori_loop(0, NP, first, 0)

    def beside1(part):
        if part == 1:

            def add(p, carry):
                amp[p] = amp[p] + delta[p]
                return carry

            lax.fori_loop(0, NP, add, 0)

    exchange(1, delta, rcv1, beside1)
    couple(plan, weight, corr, rcv1, term)

    def second(p, carry):
        s = term[plan[3, p]]
        n = cnt[p]
        amp[p] = amp[p] + s * inv[p]
        inv[p] = jnp.where((rows < n) & (cols < n), -s, 0.0)
        return carry

    lax.fori_loop(0, NP, second, 0)
    outs = [pltpu.make_async_copy(amp, amp_out, ls.at[0]), pltpu.make_async_copy(inv, res_out, ls.at[1])]
    for c in outs:
        c.start()
    for c in outs:
        c.wait()


def iterate(qi, qj, plan, weight, occ, cnt, eo, en, amp, ci, cj):
    smem = pl.BlockSpec(memory_space=pltpu.SMEM)
    vmem = pl.BlockSpec(memory_space=pltpu.VMEM)
    anyw = pl.BlockSpec(memory_space=pl.ANY)
    dma = pltpu.SemaphoreType.DMA
    mats = lambda *n: pltpu.VMEM(n + (128, 128), f32)
    return pl.pallas_call(
        iterate_kernel,
        out_shape=(jax.ShapeDtypeStruct((NP, 128, 128), f32),) * 2,
        in_specs=[smem] * 7 + [vmem] + [anyw] * 3,
        out_specs=(anyw, anyw),
        scratch_shapes=[
            mats(NP),
            mats(NP),
            mats(NC),
            mats(NP),
            mats(NC + 1),
            mats(2, 7 * CAPI),
            mats(2, 2, 4, 2 * CAPJ),
            mats(2, 2, 4, 2 * CAPJ),
            mats(SLOTS),
            mats(SLOTS),
            dma((3,)),
            dma((2, 7)),
            dma((2, 7)),
            dma((2, 2, 4, 4)),
            dma((2, 2, 4, 4)),
        ],
        compiler_params=pltpu.CompilerParams(collective_id=1, has_side_effects=True, vmem_limit_bytes=VMEM_ALL),
    )(qi, qj, plan, weight, occ, cnt, eo, en, amp, ci, cj)


def row(i_list, j_list, fill):
    rest = jnp.full((128 - 64,), fill, f32)
    return jnp.concatenate([i_list.astype(f32), j_list.astype(f32), rest])


def local(
    factors, pno_vecs, pair_occ, pno_count, pno_energy, occ_energy,
    coupi_peer, coupi_slot, coupi_target, coupi_fock, coupi_correlation,
    coupj_peer, coupj_slot, coupj_target, coupj_fock, coupj_correlation,
):
    none = jnp.zeros((128,), f32)
    tab = jnp.stack(
        [
            row(coupi_peer[:, 0], coupj_peer[:, 0] + NI, -1.0),
            row(coupi_slot, coupj_slot, 0.0),
            row(coupi_target, coupj_target, 1000.0),
            row(coupi_fock, coupj_fock, 0.0),
            none, none, none, none,
        ]
    )
    occ = pair_occ.T
    amp, qi, qj, plan, weight = integrals(occ, pno_count, occ_energy, tab, pno_energy, factors, pno_vecs)
    return iterate(
        qi, qj, plan, weight, occ, pno_count, occ_energy, pno_energy, amp, coupi_correlation, coupj_correlation
    )


def solution(mesh):
    both = ("occi", "occj")
    three, two, one = P(both, None, None), P(both, None), P(both)
    placed = (
        three, three, two, one, two, P(),
        two, one, one, one, three,
        two, one, one, one, three,
    )
    return jax.shard_map(local, mesh=mesh, in_specs=placed, out_specs=(three, three), check_vma=False)
```

```python
import functools

import jax
import jax.numpy as jnp
from jax import lax
from jax.experimental import pallas as pl
from jax.experimental.pallas import tpu as pltpu
from jax.sharding import PartitionSpec as P

MESH = pl.DeviceIdType.MESH
f32 = jnp.float32
bf16 = jnp.bfloat16
NI, NJ = 8, 16
CAPI, CAPJ = 8, 4
NP = 64
NC = 64
WAVES = 2
ROWS = 512 // WAVES
VMEM_ALL = 60 * 2**20
GROUP = 8

OFF_I = [(2, 0), (2, 1), (1, 0), (3, 0), (1, 1), (3, 1), (0, 1)]
OFF_J = sorted(
    [(a, b) for a in range(4) for b in range(4) if (a, b) != (0, 0)],
    key=lambda t: -(min(t[0], 4 - t[0]) + min(t[1], 4 - t[1])),
)


def split(x):
    hi = x.astype(bf16)
    return hi, (x - hi.astype(f32)).astype(bf16)


def dot(a, b):
    return jnp.dot(a, b, preferred_element_type=f32)


def dot_t(a, b):
    return lax.dot_general(a, b, (((1,), (1,)), ((), ())), preferred_element_type=f32)


def peer_i(u, off):
    return ((u // 2 + off[0]) % 4) * 2 + (u % 2 + off[1]) % 2


def peer_j(v, off):
    return ((v // 4 + off[0]) % 4) * 4 + (v % 4 + off[1]) % 4


def back(off, sizes):
    return tuple((n - o) % n for o, n in zip(off, sizes))


def greet(u, v):
    barrier = pltpu.get_barrier_semaphore()
    for off in OFF_I:
        pl.semaphore_signal(barrier, inc=1, device_id={"occi": peer_i(u, off)}, device_id_type=MESH)
    for off in OFF_J:
        pl.semaphore_signal(barrier, inc=1, device_id={"occj": peer_j(v, off)}, device_id_type=MESH)
    pl.semaphore_wait(barrier, len(OFF_I) + len(OFF_J))


def tables(tab, ri, rj, plan, weight):
    lane = lax.broadcasted_iota(jnp.int32, (NC, 128), 1)
    sub = lax.broadcasted_iota(jnp.int32, (NC, 128), 0)

    def across(r):
        return jnp.broadcast_to(tab[pl.ds(r, 1), :], (128, 128))

    def down(r):
        return jnp.transpose(across(r))[:NC]

    def count(mask, axis):
        return jnp.sum(jnp.where(mask, 1.0, 0.0), axis=axis, keepdims=True)

    def pick(mask, value):
        return jnp.sum(jnp.where(mask, value, 0.0), axis=0, keepdims=True)

    peer, slot, target, fock = down(0), down(1), down(2), down(3)
    rank = count((across(0)[:NC] == peer) & (lane < sub), 1)
    at = rank.astype(jnp.int32)
    for p in range(NI):
        ri[p] = pick((peer == p) & (at == lane), slot).astype(jnp.int32)
    for p in range(NJ):
        rj[p] = pick((peer == NI + p) & (at == lane), slot).astype(jnp.int32)
    arrival = jnp.where(peer < NI, peer * CAPI, NI * CAPI + (peer - NI) * CAPJ) + rank
    row_t = across(2)[:NC]
    equal = row_t == target
    place = count((row_t < target) | (equal & (lane < sub)), 1).astype(jnp.int32)
    goes_on = jnp.minimum(count(equal & (lane < sub), 1), 1.0)
    here = place == lane
    plan[pl.ds(0, 1), :] = pick(here, sub.astype(f32)).astype(jnp.int32)
    plan[pl.ds(1, 1), :] = pick(here, arrival).astype(jnp.int32)
    plan[pl.ds(2, 1), :] = pick(here, goes_on).astype(jnp.int32)
    lane_f = lane.astype(f32)
    upto = count(target <= lane_f, 0)
    plan[pl.ds(3, 1), :] = jnp.where(count(target == lane_f, 0) > 0.5, upto - 1.0, float(NC)).astype(jnp.int32)
    weight[...] = pick(here, fock)


def integral_kernel(
    occ, cnt, eo, tab, en, fac, vecs, amp, qi, qj, plan, weight,
    fi0, fi1, fj0, fj1, th0, th1, tl0, tl1, jh0, jh1, jl0, jl1, vec, both, acc, ri, rj, own_sem, tab_sem, rs, ss, crs, css, out_sem,
):
    u = lax.axis_index("occi")
    v = lax.axis_index("occj")
    x, z = v % 4, v // 4
    y, core = u // 2, u % 2
    fi, fj = (fi0, fi1), (fj0, fj1)
    th, tl, jh, jl = (th0, th1), (tl0, tl1), (jh0, jh1), (jl0, jl1)

    def vid(zz, xx):
        return ((z + zz) % 4) * 4 + (x + xx) % 4

    def uid(yy, cc):
        return ((y + yy) % 4) * 2 + (core + cc) % 2

    own = [pltpu.make_async_copy(vecs, vec, own_sem.at[0])]
    for w in range(WAVES):
        at = fac.at[0, pl.ds(w * ROWS, ROWS)]
        own.append(pltpu.make_async_copy(at, fi[w].at[v], own_sem.at[1 + 2 * w]))
        own.append(pltpu.make_async_copy(at, fj[w].at[u], own_sem.at[2 + 2 * w]))
    greet(u, v)
    for c in own:
        c.start()
    pending = []

    def send(w, from_fac, buf, slot, q, n, sem, dev):
        at = buf[w].at[slot, pl.ds(q, n)]
        src = fac.at[0, pl.ds(w * ROWS + q, n)] if from_fac else at
        c = pltpu.make_async_remote_copy(src, at, sem[0], sem[1], dev, MESH)
        c.start()
        pending.append(c)

    def got(w, buf, slot, q, n, sem, dev):
        at = buf[w].at[slot, pl.ds(q, n)]
        pltpu.make_async_remote_copy(at, at, sem[0], sem[1], dev, MESH).wait_recv()

    def wave(w):
        h = ROWS // 2
        s = h // 2

        def sem(half, k):
            return ss.at[w, half, k], rs.at[w, half, k]

        def csem(k):
            return css.at[w, k], crs.at[w, k]

        halves = []
        for half in (0, 1):
            if half == 0:
                first = lambda d: {"occj": vid(0, d)}
                second = lambda d: {"occj": vid(d, 0)}
                slot = lambda a, b: vid(b, a)
            else:
                first = lambda d: {"occj": vid(d, 0)}
                second = lambda d: {"occj": vid(0, d)}
                slot = lambda a, b: vid(a, b)
            halves.append((half, half * h, first, second, slot))

        def second_send(half, q, second, slot, a, base, mine=False):
            send(w, mine, fi, slot(a, 0), q, h, sem(half, base), second(1))
            send(w, mine, fi, slot(a, 0), q, h, sem(half, base + 1), second(3))

        def second_forward(half, q, second, slot, a, base):
            got(w, fi, slot(a, 3), q, h, sem(half, base), second(1))
            send(w, False, fi, slot(a, 3), q, s, sem(half, base + 2), second(1))
            got(w, fi, slot(a, 1), q, h, sem(half, base + 1), second(1))
            send(w, False, fi, slot(a, 1), q + s, s, sem(half, base + 3), second(3))

        def s0():
            for half, q, first, second, slot in halves:
                send(w, True, fi, v, q, h, sem(half, 0), first(1))
                send(w, True, fi, v, q, h, sem(half, 1), first(3))
            for half, q, first, second, slot in halves:
                second_send(half, q, second, slot, 0, 4, True)
            send(w, True, fj, u, 0, ROWS, csem(0), {"occi": uid(1, 0)})
            send(w, True, fj, u, 0, ROWS, csem(1), {"occi": uid(3, 0)})
            send(w, True, fj, u, 0, ROWS, csem(4), {"occi": uid(0, 1)})

        def s1():
            for half, q, first, second, slot in halves:
                got(w, fi, slot(3, 0), q, h, sem(half, 0), first(1))
                send(w, False, fi, slot(3, 0), q, s, sem(half, 2), first(1))
                got(w, fi, slot(1, 0), q, h, sem(half, 1), first(1))
                send(w, False, fi, slot(1, 0), q + s, s, sem(half, 3), first(3))
            for half, q, first, second, slot in halves:
                second_send(half, q, second, slot, 3, 8)
                second_send(half, q, second, slot, 1, 12)

        def s2():
            for half, q, first, second, slot in halves:
                second_forward(half, q, second, slot, 0, 4)
            n = ROWS // 2
            got(w, fj, uid(3, 0), 0, ROWS, csem(0), {"occi": uid(1, 0)})
            send(w, False, fj, uid(3, 0), 0, n, csem(2), {"occi": uid(1, 0)})
            send(w, False, fj, uid(3, 0), 0, ROWS, csem(5), {"occi": uid(0, 1)})
            got(w, fj, uid(1, 0), 0, ROWS, csem(1), {"occi": uid(1, 0)})
            send(w, False, fj, uid(1, 0), n, n, csem(3), {"occi": uid(3, 0)})
            send(w, False, fj, uid(1, 0), 0, ROWS, csem(6), {"occi": uid(0, 1)})

        def s3():
            for half, q, first, second, slot in halves:
                got(w, fi, slot(2, 0), q, s, sem(half, 2), first(1))
                got(w, fi, slot(2, 0), q + s, s, sem(half, 3), first(1))
                second_send(half, q, second, slot, 2, 16)

        def s4():
            for half, q, first, second, slot in halves:
                second_forward(half, q, second, slot, 3, 8)
                second_forward(half, q, second, slot, 1, 12)
            n = ROWS // 2
            got(w, fj, uid(2, 0), 0, n, csem(2), {"occi": uid(1, 0)})
            got(w, fj, uid(2, 0), n, n, csem(3), {"occi": uid(1, 0)})
            send(w, False, fj, uid(2, 0), 0, ROWS, csem(7), {"occi": uid(0, 1)})

        def s5():
            for half, q, first, second, slot in halves:
                second_forward(half, q, second, slot, 2, 16)

        def s6():
            for half, q, first, second, slot in halves:
                for a, base in ((0, 4), (3, 8), (1, 12), (2, 16)):
                    got(w, fi, slot(a, 2), q, s, sem(half, base + 2), second(1))
                    got(w, fi, slot(a, 2), q + s, s, sem(half, base + 3), second(1))
            for k, yy in ((4, 0), (5, 3), (6, 1), (7, 2)):
                got(w, fj, uid(yy, 1), 0, ROWS, csem(k), {"occi": uid(0, 1)})

        return s0, s1, s2, s3, s4, s5, s6

    def halve_i(w, blocks):
        for dz, dx in blocks:
            k = vid(dz, dx)
            th[w][k], tl[w][k] = split(fi[w][k])

    def halve_j(w):
        def body(k, c):
            jh[w][k], jl[w][k] = split(fj[w][k])
            return c

        lax.fori_loop(0, NI, body, 0)

    def halve_vectors():
        def body(b, c):
            for k in range(2):
                h, l = split(vec[2 * b + k])
                both[2 * b + k] = jnp.concatenate([h, l], axis=1)
            return c

        lax.fori_loop(0, NP // 2, body, 0)

    rows = lax.broadcasted_iota(jnp.int32, (128, 128), 0)
    cols = lax.broadcasted_iota(jnp.int32, (128, 128), 1)

    def some(w, lo, hi):
        def body(b, c):
            group = [b * GROUP + g for g in range(GROUP)]
            stage = []
            for p in group:
                i, j = lax.rem(occ[0, p], NJ), lax.div(occ[1, p], NJ)
                hl = both[p]
                h = hl[:, :128]
                one = dot(th[w][i], hl)
                left = one[:, :128] + one[:, 128:] + dot(tl[w][i], h)
                two = dot(jh[w][j], hl)
                right = two[:, :128] + two[:, 128:] + dot(jl[w][j], h)
                stage.append((left, right))
            stage = [
                (jnp.concatenate(split(left), axis=1), jnp.concatenate(split(right), axis=1)) for left, right in stage
            ]
            stage = [dot_0(left, right) for left, right in stage]
            stage = [(o[:128, :128] + o[:128, 128:]) + o[128:, :128] for o in stage]
            if w == 0:
                for p, o in zip(group, stage):
                    acc[p] = o
                return c
            sums = [denominator(en, p) for p in group]
            for p, o, den in zip(group, stage, sums):
                den = den - (eo[occ[0, p]] + eo[occ[1, p]])
                n = cnt[p]
                acc[p] = jnp.where((rows < n) & (cols < n), -(acc[p] + o) / den, 0.0)
            return c

        lax.fori_loop(lo // GROUP, hi // GROUP, body, 0)

    near = [(0, 0), (0, 1), (0, 3), (1, 0), (3, 0)]
    middle = [(1, 1), (1, 3), (3, 1), (3, 3)]
    far = [(0, 2), (2, 0), (1, 2), (3, 2), (2, 1), (2, 3), (2, 2)]
    a, b = wave(0), wave(1)
    a[0]()
    tables(tab, ri, rj, plan, weight)
    waits = []
    for k, off in enumerate(OFF_I + OFF_J):
        if k < 7:
            to, frm, me, r, q, name = peer_i(u, off), peer_i(u, back(off, (4, 2))), u, ri, qi, "occi"
        else:
            to, frm, me, r, q, name = peer_j(v, off), peer_j(v, back(off, (4, 4))), v, rj, qj, "occj"
        c = pltpu.make_async_remote_copy(r.at[to], q.at[me], tab_sem.at[0, k], tab_sem.at[1, k], {name: to}, MESH)
        c.start()
        pending.append(c)
        waits.append(
            pltpu.make_async_remote_copy(r.at[frm], q.at[frm], tab_sem.at[0, k], tab_sem.at[1, k], {name: to}, MESH)
        )
    qi[u] = ri[u]
    qj[v] = rj[v]
    a[1]()
    b[0]()
    own[0].wait()
    halve_vectors()
    a[2]()
    a[3]()
    b[1]()
    for c in own[1:]:
        c.wait()
    halve_i(0, near)
    a[4]()
    b[2]()
    halve_i(1, near)
    a[5]()
    b[3]()
    halve_i(0, middle)
    a[6]()
    halve_i(0, far)
    halve_j(0)
    some(0, 0, 16)
    b[4]()
    some(0, 16, 32)
    b[5]()
    halve_i(1, middle)
    some(0, 32, 64)
    b[6]()
    halve_i(1, far)
    halve_j(1)
    outs = []
    for k in range(4):
        some(1, 16 * k, 16 * k + 16)
        part = pl.ds(16 * k, 16)
        c = pltpu.make_async_copy(acc.at[part], amp.at[part], out_sem.at[k])
        c.start()
        outs.append(c)
    for c in waits:
        c.wait_recv()
    for c in pending:
        c.wait_send()
    for c in outs:
        c.wait()


def dot_0(a, b):
    return lax.dot_general(a, b, (((0,), (0,)), ((), ())), preferred_element_type=f32)


def denominator(en, p):
    across = jnp.broadcast_to(en[pl.ds(p, 1), :], (128, 128))
    return jnp.transpose(across) + across


def integrals(occ, cnt, eo, tab, en, factors, vecs):
    smem = pl.BlockSpec(memory_space=pltpu.SMEM)
    vmem = pl.BlockSpec(memory_space=pltpu.VMEM)
    anyw = pl.BlockSpec(memory_space=pl.ANY)
    i32 = jnp.int32
    dma = pltpu.SemaphoreType.DMA
    return pl.pallas_call(
        integral_kernel,
        out_shape=(
            jax.ShapeDtypeStruct((NP, 128, 128), f32),
            jax.ShapeDtypeStruct((NI, 1, 128), i32),
            jax.ShapeDtypeStruct((NJ, 1, 128), i32),
            jax.ShapeDtypeStruct((8, 128), i32),
            jax.ShapeDtypeStruct((1, 128), f32),
        ),
        in_specs=[smem] * 3 + [vmem] * 2 + [anyw] * 2,
        out_specs=(anyw, vmem, vmem, vmem, vmem),
        scratch_shapes=[
            pltpu.VMEM((NJ, ROWS, 256), f32),
            pltpu.VMEM((NJ, ROWS, 256), f32),
            pltpu.VMEM((NI, ROWS, 256), f32),
            pltpu.VMEM((NI, ROWS, 256), f32),
            *[pltpu.VMEM((NJ, ROWS, 256), bf16)] * 4,
            *[pltpu.VMEM((NI, ROWS, 256), bf16)] * 4,
            pltpu.VMEM((NP, 256, 128), f32),
            pltpu.VMEM((NP, 256, 256), bf16),
            pltpu.VMEM((NP, 128, 128), f32),
            pltpu.VMEM((NI, 1, 128), i32),
            pltpu.VMEM((NJ, 1, 128), i32),
            dma((5,)),
            dma((2, 22)),
            dma((WAVES, 2, 20)),
            dma((WAVES, 2, 20)),
            dma((WAVES, 8)),
            dma((WAVES, 8)),
            dma((4,)),
        ],
        compiler_params=pltpu.CompilerParams(collective_id=0, has_side_effects=True, vmem_limit_bytes=VMEM_ALL),
    )(occ, cnt, eo, tab, en, factors, vecs)


UNROLL = 8
SLOTS = NI * CAPI + NJ * CAPJ


def couple(plan, weight, corr, arrived, term):
    term[NC] = jnp.zeros((128, 128), f32)

    def body(b, run):
        places = [b * UNROLL + k for k in range(UNROLL)]
        corrs = [split(corr[plan[0, s]]) for s in places]
        stage = []
        for s, (mh, ml) in zip(places, corrs):
            xh, xl = split(arrived[plan[1, s]])
            xx = jnp.concatenate([xh, xl], axis=1)
            stage.append((jnp.concatenate([mh, ml], axis=1), jnp.concatenate([xx, xx], axis=0)))
        stage = [dot(m, x) for m, x in stage]
        stage = [jnp.concatenate(split(h[:, :128] + h[:, 128:]), axis=1) for h in stage]
        corrs = [
            jnp.concatenate([jnp.concatenate([mh, mh], axis=1), jnp.concatenate([ml, ml], axis=1)], axis=0)
            for mh, ml in corrs
        ]
        stage = [dot_t(h, m) for h, m in zip(stage, corrs)]
        for s, t in zip(places, stage):
            t = (t[:, :128] + t[:, 128:]) * weight[0, s]
            run = jnp.where(plan[2, s] > 0, run, 0.0) + t
            term[s] = run
        return run

    lax.fori_loop(0, NC // UNROLL, body, jnp.zeros((128, 128), f32))


def iterate_kernel(
    qi, qj, plan, weight, occ, cnt, eo, en, amp0, ci, cj, amp_out, res_out,
    amp, inv, corr, delta, term, snd_i, snd_j, mid, rcv0, rcv1, ls, si, ri, sj, rj,
):
    u = lax.axis_index("occi")
    v = lax.axis_index("occj")
    x, z = v % 4, v // 4
    rows = lax.broadcasted_iota(jnp.int32, (128, 128), 0)
    cols = lax.broadcasted_iota(jnp.int32, (128, 128), 1)
    loads = [
        pltpu.make_async_copy(amp0, amp, ls.at[0]),
        pltpu.make_async_copy(ci, corr.at[pl.ds(0, 32)], ls.at[1]),
        pltpu.make_async_copy(cj, corr.at[pl.ds(32, 32)], ls.at[2]),
    ]
    for c in loads:
        c.start()
    greet(u, v)

    def vid(dz, dx):
        return ((z + dz) % 4) * 4 + (x + dx) % 4

    def exchange(it, src, arrived, beside):
        half_rows = CAPJ // 2
        first, rest, sent = {}, [], []

        def fill(half, d):
            for e in range(4):
                if d == 0 and e == 0:
                    continue
                to = vid(e, d) if half == 0 else vid(d, e)
                for s in range(half_rows):
                    snd_j[it, half, d, half_rows * e + s] = src[qj[to, 0, half_rows * half + s]]

        def place(half, d, e):
            frm = vid((4 - e) % 4, (4 - d) % 4) if half == 0 else vid((4 - d) % 4, (4 - e) % 4)
            return arrived.at[pl.ds(NI * CAPI + frm * CAPJ + half_rows * half, half_rows)]

        for d in (2, 1, 3):
            for half in (0, 1):
                fill(half, d)
                to = vid(0, d) if half == 0 else vid(d, 0)
                c = pltpu.make_async_remote_copy(
                    snd_j.at[it, half, d], mid.at[it, half, d], sj.at[it, half, d, 0], rj.at[it, half, d, 0], {"occj": to}, MESH
                )
                c.start()
                first[half, d] = c
                sent.append(c)
        for k, off in enumerate(OFF_I):
            to, frm = peer_i(u, off), peer_i(u, back(off, (4, 2)))
            for s in range(CAPI):
                snd_i[it, k * CAPI + s] = src[qi[to, 0, s]]
            out = snd_i.at[it, pl.ds(k * CAPI, CAPI)]
            c = pltpu.make_async_remote_copy(
                out, arrived.at[pl.ds(u * CAPI, CAPI)], si.at[it, k], ri.at[it, k], {"occi": to}, MESH
            )
            c.start()
            sent.append(c)
            rest.append(
                pltpu.make_async_remote_copy(
                    out, arrived.at[pl.ds(frm * CAPI, CAPI)], si.at[it, k], ri.at[it, k], {"occi": to}, MESH
                )
            )

        def onward(half, d):
            for e in (2, 1, 3):
                to = vid(e, 0) if half == 0 else vid(0, e)
                out = (snd_j if d == 0 else mid).at[it, half, d, pl.ds(half_rows * e, half_rows)]
                start = vid(0, (4 - d) % 4) if half == 0 else vid((4 - d) % 4, 0)
                into = arrived.at[pl.ds(NI * CAPI + start * CAPJ + half_rows * half, half_rows)]
                c = pltpu.make_async_remote_copy(
                    out, into, sj.at[it, half, d, e], rj.at[it, half, d, e], {"occj": to}, MESH
                )
                c.start()
                sent.append(c)
                rest.append(
                    pltpu.make_async_remote_copy(
                        out, place(half, d, e), sj.at[it, half, d, e], rj.at[it, half, d, e], {"occj": to}, MESH
                    )
                )

        for half in (0, 1):
            fill(half, 0)
            onward(half, 0)
        for s in range(CAPI):
            arrived[u * CAPI + s] = src[qi[u, 0, s]]
        for s in range(CAPJ):
            arrived[NI * CAPI + v * CAPJ + s] = src[qj[v, 0, s]]
        beside(0)
        for d in (1, 3, 2):
            for half in (0, 1):
                first[half, d].wait_recv()
                onward(half, d)
            if d == 3:
                beside(1)
        for half in (0, 1):
            for d in (1, 3, 2):
                frm = vid(0, (4 - d) % 4) if half == 0 else vid((4 - d) % 4, 0)
                for s in range(half_rows):
                    arrived[NI * CAPI + frm * CAPJ + half_rows * half + s] = mid[it, half, d, s]
        beside(2)
        for c in rest:
            c.wait_recv()
        for c in sent:
            c.wait_send()

    def inverses(lo, hi):
        def body(p, carry):
            den = denominator(en, p) - (eo[occ[0, p]] + eo[occ[1, p]])
            n = cnt[p]
            inv[p] = jnp.where((rows < n) & (cols < n), 1.0 / den, 0.0)
            return carry

        lax.fori_loop(lo, hi, body, 0)

    def beside0(part):
        if part == 0:
            inverses(0, 16)
        elif part == 1:
            inverses(16, 32)
        else:
            inverses(32, 64)
            for c in loads[1:]:
                c.wait()

    loads[0].wait()
    exchange(0, amp, rcv0, beside0)
    couple(plan, weight, corr, rcv0, term)

    def first(b, carry):
        for k in range(4):
            p = 4 * b + k
            delta[p] = term[plan[3, p]] * inv[p]
        return carry

    lax.fori_loop(0, NP // 4, first, 0)

    def beside1(part):
        if part == 1:

            def add(p, carry):
                amp[p] = amp[p] + delta[p]
                return carry

            lax.fori_loop(0, NP, add, 0)

    exchange(1, delta, rcv1, beside1)
    couple(plan, weight, corr, rcv1, term)

    def second(b, carry):
        for k in range(4):
            p = 4 * b + k
            s = term[plan[3, p]]
            n = cnt[p]
            amp[p] = amp[p] + s * inv[p]
            inv[p] = jnp.where((rows < n) & (cols < n), -s, 0.0)
        return carry

    lax.fori_loop(0, NP // 4, second, 0)
    outs = [pltpu.make_async_copy(amp, amp_out, ls.at[0]), pltpu.make_async_copy(inv, res_out, ls.at[1])]
    for c in outs:
        c.start()
    for c in outs:
        c.wait()


def iterate(qi, qj, plan, weight, occ, cnt, eo, en, amp, ci, cj):
    smem = pl.BlockSpec(memory_space=pltpu.SMEM)
    vmem = pl.BlockSpec(memory_space=pltpu.VMEM)
    anyw = pl.BlockSpec(memory_space=pl.ANY)
    dma = pltpu.SemaphoreType.DMA
    mats = lambda *n: pltpu.VMEM(n + (128, 128), f32)
    return pl.pallas_call(
        iterate_kernel,
        out_shape=(jax.ShapeDtypeStruct((NP, 128, 128), f32),) * 2,
        in_specs=[smem] * 7 + [vmem] + [anyw] * 3,
        out_specs=(anyw, anyw),
        scratch_shapes=[
            mats(NP),
            mats(NP),
            mats(NC),
            mats(NP),
            mats(NC + 1),
            mats(2, 7 * CAPI),
            mats(2, 2, 4, 2 * CAPJ),
            mats(2, 2, 4, 2 * CAPJ),
            mats(SLOTS),
            mats(SLOTS),
            dma((3,)),
            dma((2, 7)),
            dma((2, 7)),
            dma((2, 2, 4, 4)),
            dma((2, 2, 4, 4)),
        ],
        compiler_params=pltpu.CompilerParams(collective_id=1, has_side_effects=True, vmem_limit_bytes=VMEM_ALL),
    )(qi, qj, plan, weight, occ, cnt, eo, en, amp, ci, cj)


def row(i_list, j_list, fill):
    rest = jnp.full((128 - 64,), fill, f32)
    return jnp.concatenate([i_list.astype(f32), j_list.astype(f32), rest])


def local(
    factors, pno_vecs, pair_occ, pno_count, pno_energy, occ_energy,
    coupi_peer, coupi_slot, coupi_target, coupi_fock, coupi_correlation,
    coupj_peer, coupj_slot, coupj_target, coupj_fock, coupj_correlation,
):
    none = jnp.zeros((128,), f32)
    tab = jnp.stack(
        [
            row(coupi_peer[:, 0], coupj_peer[:, 0] + NI, -1.0),
            row(coupi_slot, coupj_slot, 0.0),
            row(coupi_target, coupj_target, 1000.0),
            row(coupi_fock, coupj_fock, 0.0),
            none, none, none, none,
        ]
    )
    occ = pair_occ.T
    amp, qi, qj, plan, weight = integrals(occ, pno_count, occ_energy, tab, pno_energy, factors, pno_vecs)
    return iterate(
        qi, qj, plan, weight, occ, pno_count, occ_energy, pno_energy, amp, coupi_correlation, coupj_correlation
    )


def solution(mesh):
    both = ("occi", "occj")
    three, two, one = P(both, None, None), P(both, None), P(both)
    placed = (
        three, three, two, one, two, P(),
        two, one, one, one, three,
        two, one, one, one, three,
    )
    return jax.shard_map(local, mesh=mesh, in_specs=placed, out_specs=(three, three), check_vma=False)
```

```python
import functools

import jax
import jax.numpy as jnp
from jax import lax
from jax.experimental import pallas as pl
from jax.experimental.pallas import tpu as pltpu
from jax.sharding import PartitionSpec as P

MESH = pl.DeviceIdType.MESH
f32 = jnp.float32
bf16 = jnp.bfloat16
NI, NJ = 8, 16
CAPI, CAPJ = 8, 4
NP = 64
NC = 64
WAVES = 2
ROWS = 512 // WAVES
VMEM_ALL = 60 * 2**20
GROUP = 8

OFF_I = [(2, 0), (2, 1), (1, 0), (3, 0), (1, 1), (3, 1), (0, 1)]
OFF_J = sorted(
    [(a, b) for a in range(4) for b in range(4) if (a, b) != (0, 0)],
    key=lambda t: -(min(t[0], 4 - t[0]) + min(t[1], 4 - t[1])),
)


def split(x):
    hi = x.astype(bf16)
    return hi, (x - hi.astype(f32)).astype(bf16)


def dot(a, b):
    return jnp.dot(a, b, preferred_element_type=f32)


def dot_t(a, b):
    return lax.dot_general(a, b, (((1,), (1,)), ((), ())), preferred_element_type=f32)


def peer_i(u, off):
    return ((u // 2 + off[0]) % 4) * 2 + (u % 2 + off[1]) % 2


def peer_j(v, off):
    return ((v // 4 + off[0]) % 4) * 4 + (v % 4 + off[1]) % 4


def back(off, sizes):
    return tuple((n - o) % n for o, n in zip(off, sizes))


def greet(u, v):
    barrier = pltpu.get_barrier_semaphore()
    for off in OFF_I:
        pl.semaphore_signal(barrier, inc=1, device_id={"occi": peer_i(u, off)}, device_id_type=MESH)
    for off in OFF_J:
        pl.semaphore_signal(barrier, inc=1, device_id={"occj": peer_j(v, off)}, device_id_type=MESH)
    pl.semaphore_wait(barrier, len(OFF_I) + len(OFF_J))


def tables(tab, ri, rj, plan, weight):
    lane = lax.broadcasted_iota(jnp.int32, (NC, 128), 1)
    sub = lax.broadcasted_iota(jnp.int32, (NC, 128), 0)

    def across(r):
        return jnp.broadcast_to(tab[pl.ds(r, 1), :], (128, 128))

    def down(r):
        return jnp.transpose(across(r))[:NC]

    def count(mask, axis):
        return jnp.sum(jnp.where(mask, 1.0, 0.0), axis=axis, keepdims=True)

    def pick(mask, value):
        return jnp.sum(jnp.where(mask, value, 0.0), axis=0, keepdims=True)

    peer, slot, target, fock = down(0), down(1), down(2), down(3)
    rank = count((across(0)[:NC] == peer) & (lane < sub), 1)
    at = rank.astype(jnp.int32)
    for p in range(NI):
        ri[p] = pick((peer == p) & (at == lane), slot).astype(jnp.int32)
    for p in range(NJ):
        rj[p] = pick((peer == NI + p) & (at == lane), slot).astype(jnp.int32)
    arrival = jnp.where(peer < NI, peer * CAPI, NI * CAPI + (peer - NI) * CAPJ) + rank
    row_t = across(2)[:NC]
    equal = row_t == target
    place = count((row_t < target) | (equal & (lane < sub)), 1).astype(jnp.int32)
    goes_on = jnp.minimum(count(equal & (lane < sub), 1), 1.0)
    here = place == lane
    plan[pl.ds(0, 1), :] = pick(here, sub.astype(f32)).astype(jnp.int32)
    plan[pl.ds(1, 1), :] = pick(here, arrival).astype(jnp.int32)
    plan[pl.ds(2, 1), :] = pick(here, goes_on).astype(jnp.int32)
    lane_f = lane.astype(f32)
    upto = count(target <= lane_f, 0)
    plan[pl.ds(3, 1), :] = jnp.where(count(target == lane_f, 0) > 0.5, upto - 1.0, float(NC)).astype(jnp.int32)
    weight[...] = pick(here, fock)


def integral_kernel(
    occ, cnt, eo, pi, pj, si, sj, ti, tj, ki, kj, en, fac, vecs, amp, qi, qj, plan, weight,
    fi0, fi1, fj0, fj1, th0, th1, tl0, tl1, jh0, jh1, jl0, jl1, vec, both, acc, tab, ri, rj, own_sem, tab_sem, rs, ss, crs, css, out_sem,
):
    u = lax.axis_index("occi")
    v = lax.axis_index("occj")
    x, z = v % 4, v // 4
    y, core = u // 2, u % 2
    fi, fj = (fi0, fi1), (fj0, fj1)
    th, tl, jh, jl = (th0, th1), (tl0, tl1), (jh0, jh1), (jl0, jl1)

    def vid(zz, xx):
        return ((z + zz) % 4) * 4 + (x + xx) % 4

    def uid(yy, cc):
        return ((y + yy) % 4) * 2 + (core + cc) % 2

    own = [pltpu.make_async_copy(vecs, vec, own_sem.at[0])]
    for w in range(WAVES):
        at = fac.at[0, pl.ds(w * ROWS, ROWS)]
        own.append(pltpu.make_async_copy(at, fi[w].at[v], own_sem.at[1 + 2 * w]))
        own.append(pltpu.make_async_copy(at, fj[w].at[u], own_sem.at[2 + 2 * w]))
    greet(u, v)
    for c in own:
        c.start()
    pending = []

    def send(w, from_fac, buf, slot, q, n, sem, dev):
        at = buf[w].at[slot, pl.ds(q, n)]
        src = fac.at[0, pl.ds(w * ROWS + q, n)] if from_fac else at
        c = pltpu.make_async_remote_copy(src, at, sem[0], sem[1], dev, MESH)
        c.start()
        pending.append(c)

    def got(w, buf, slot, q, n, sem, dev):
        at = buf[w].at[slot, pl.ds(q, n)]
        pltpu.make_async_remote_copy(at, at, sem[0], sem[1], dev, MESH).wait_recv()

    def wave(w):
        h = ROWS // 2
        s = h // 2

        def sem(half, k):
            return ss.at[w, half, k], rs.at[w, half, k]

        def csem(k):
            return css.at[w, k], crs.at[w, k]

        halves = []
        for half in (0, 1):
            if half == 0:
                first = lambda d: {"occj": vid(0, d)}
                second = lambda d: {"occj": vid(d, 0)}
                slot = lambda a, b: vid(b, a)
            else:
                first = lambda d: {"occj": vid(d, 0)}
                second = lambda d: {"occj": vid(0, d)}
                slot = lambda a, b: vid(a, b)
            halves.append((half, half * h, first, second, slot))

        def second_send(half, q, second, slot, a, base, mine=False):
            send(w, mine, fi, slot(a, 0), q, h, sem(half, base), second(1))
            send(w, mine, fi, slot(a, 0), q, h, sem(half, base + 1), second(3))

        def second_forward(half, q, second, slot, a, base):
            got(w, fi, slot(a, 3), q, h, sem(half, base), second(1))
            send(w, False, fi, slot(a, 3), q, s, sem(half, base + 2), second(1))
            got(w, fi, slot(a, 1), q, h, sem(half, base + 1), second(1))
            send(w, False, fi, slot(a, 1), q + s, s, sem(half, base + 3), second(3))

        def s0():
            for half, q, first, second, slot in halves:
                send(w, True, fi, v, q, h, sem(half, 0), first(1))
                send(w, True, fi, v, q, h, sem(half, 1), first(3))
            for half, q, first, second, slot in halves:
                second_send(half, q, second, slot, 0, 4, True)
            send(w, True, fj, u, 0, ROWS, csem(0), {"occi": uid(1, 0)})
            send(w, True, fj, u, 0, ROWS, csem(1), {"occi": uid(3, 0)})
            send(w, True, fj, u, 0, ROWS, csem(4), {"occi": uid(0, 1)})

        def s1():
            for half, q, first, second, slot in halves:
                got(w, fi, slot(3, 0), q, h, sem(half, 0), first(1))
                send(w, False, fi, slot(3, 0), q, s, sem(half, 2), first(1))
                got(w, fi, slot(1, 0), q, h, sem(half, 1), first(1))
                send(w, False, fi, slot(1, 0), q + s, s, sem(half, 3), first(3))
            for half, q, first, second, slot in halves:
                second_send(half, q, second, slot, 3, 8)
                second_send(half, q, second, slot, 1, 12)

        def s2():
            for half, q, first, second, slot in halves:
                second_forward(half, q, second, slot, 0, 4)
            n = ROWS // 2
            got(w, fj, uid(3, 0), 0, ROWS, csem(0), {"occi": uid(1, 0)})
            send(w, False, fj, uid(3, 0), 0, n, csem(2), {"occi": uid(1, 0)})
            send(w, False, fj, uid(3, 0), 0, ROWS, csem(5), {"occi": uid(0, 1)})
            got(w, fj, uid(1, 0), 0, ROWS, csem(1), {"occi": uid(1, 0)})
            send(w, False, fj, uid(1, 0), n, n, csem(3), {"occi": uid(3, 0)})
            send(w, False, fj, uid(1, 0), 0, ROWS, csem(6), {"occi": uid(0, 1)})

        def s3():
            for half, q, first, second, slot in halves:
                got(w, fi, slot(2, 0), q, s, sem(half, 2), first(1))
                got(w, fi, slot(2, 0), q + s, s, sem(half, 3), first(1))
                second_send(half, q, second, slot, 2, 16)

        def s4():
            for half, q, first, second, slot in halves:
                second_forward(half, q, second, slot, 3, 8)
                second_forward(half, q, second, slot, 1, 12)
            n = ROWS // 2
            got(w, fj, uid(2, 0), 0, n, csem(2), {"occi": uid(1, 0)})
            got(w, fj, uid(2, 0), n, n, csem(3), {"occi": uid(1, 0)})
            send(w, False, fj, uid(2, 0), 0, ROWS, csem(7), {"occi": uid(0, 1)})

        def s5():
            for half, q, first, second, slot in halves:
                second_forward(half, q, second, slot, 2, 16)

        def s6():
            for half, q, first, second, slot in halves:
                for a, base in ((0, 4), (3, 8), (1, 12), (2, 16)):
                    got(w, fi, slot(a, 2), q, s, sem(half, base + 2), second(1))
                    got(w, fi, slot(a, 2), q + s, s, sem(half, base + 3), second(1))
            for k, yy in ((4, 0), (5, 3), (6, 1), (7, 2)):
                got(w, fj, uid(yy, 1), 0, ROWS, csem(k), {"occi": uid(0, 1)})

        return s0, s1, s2, s3, s4, s5, s6

    def halve_i(w, blocks):
        for dz, dx in blocks:
            k = vid(dz, dx)
            th[w][k], tl[w][k] = split(fi[w][k])

    def halve_j(w):
        def body(k, c):
            jh[w][k], jl[w][k] = split(fj[w][k])
            return c

        lax.fori_loop(0, NI, body, 0)

    def halve_vectors():
        def body(b, c):
            for k in range(2):
                h, l = split(vec[2 * b + k])
                both[2 * b + k] = jnp.concatenate([h, l], axis=1)
            return c

        lax.fori_loop(0, NP // 2, body, 0)

    rows = lax.broadcasted_iota(jnp.int32, (128, 128), 0)
    cols = lax.broadcasted_iota(jnp.int32, (128, 128), 1)

    def some(w, lo, hi):
        def body(b, c):
            group = [b * GROUP + g for g in range(GROUP)]
            stage = []
            for p in group:
                i, j = lax.rem(occ[0, p], NJ), lax.div(occ[1, p], NJ)
                hl = both[p]
                h = hl[:, :128]
                one = dot(th[w][i], hl)
                left = one[:, :128] + one[:, 128:] + dot(tl[w][i], h)
                two = dot(jh[w][j], hl)
                right = two[:, :128] + two[:, 128:] + dot(jl[w][j], h)
                stage.append((left, right))
            stage = [
                (jnp.concatenate(split(left), axis=1), jnp.concatenate(split(right), axis=1)) for left, right in stage
            ]
            stage = [dot_0(left, right) for left, right in stage]
            stage = [(o[:128, :128] + o[:128, 128:]) + o[128:, :128] for o in stage]
            if w == 0:
                for p, o in zip(group, stage):
                    acc[p] = o
                return c
            sums = [denominator(en, p) for p in group]
            for p, o, den in zip(group, stage, sums):
                den = den - (eo[occ[0, p]] + eo[occ[1, p]])
                n = cnt[p]
                acc[p] = jnp.where((rows < n) & (cols < n), -(acc[p] + o) / den, 0.0)
            return c

        lax.fori_loop(lo // GROUP, hi // GROUP, body, 0)

    near = [(0, 0), (0, 1), (0, 3), (1, 0), (3, 0)]
    middle = [(1, 1), (1, 3), (3, 1), (3, 3)]
    far = [(0, 2), (2, 0), (1, 2), (3, 2), (2, 1), (2, 3), (2, 2)]
    a, b = wave(0), wave(1)
    a[0]()
    for r, (one, two, fill) in enumerate(((pi, pj, -1.0), (si, sj, 0.0), (ti, tj, 1000.0), (ki, kj, 0.0))):
        tab[pl.ds(r, 1), :] = jnp.full((1, 128), fill, f32)
        tab[pl.ds(r, 1), 0:32] = one[...].astype(f32)
        tab[pl.ds(r, 1), 32:64] = two[...].astype(f32) + (float(NI) if r == 0 else 0.0)
    tables(tab, ri, rj, plan, weight)
    b[0]()
    waits = []
    for k, off in enumerate(OFF_I + OFF_J):
        if k < 7:
            to, frm, me, r, q, name = peer_i(u, off), peer_i(u, back(off, (4, 2))), u, ri, qi, "occi"
        else:
            to, frm, me, r, q, name = peer_j(v, off), peer_j(v, back(off, (4, 4))), v, rj, qj, "occj"
        c = pltpu.make_async_remote_copy(r.at[to], q.at[me], tab_sem.at[0, k], tab_sem.at[1, k], {name: to}, MESH)
        c.start()
        pending.append(c)
        waits.append(
            pltpu.make_async_remote_copy(r.at[frm], q.at[frm], tab_sem.at[0, k], tab_sem.at[1, k], {name: to}, MESH)
        )
    qi[u] = ri[u]
    qj[v] = rj[v]
    a[1]()
    a[2]()
    a[3]()
    own[0].wait()
    halve_vectors()
    b[1]()
    for c in own[1:]:
        c.wait()
    halve_i(0, near)
    a[4]()
    halve_i(0, middle)
    a[5]()
    b[2]()
    halve_i(1, near)
    b[3]()
    a[6]()
    halve_i(0, far)
    halve_j(0)
    some(0, 0, 16)
    b[4]()
    some(0, 16, 32)
    b[5]()
    some(0, 32, 64)
    halve_i(1, middle)
    b[6]()
    halve_i(1, far)
    halve_j(1)
    outs = []
    for k in range(4):
        some(1, 16 * k, 16 * k + 16)
        part = pl.ds(16 * k, 16)
        c = pltpu.make_async_copy(acc.at[part], amp.at[part], out_sem.at[k])
        c.start()
        outs.append(c)
    for c in waits:
        c.wait_recv()
    for c in pending:
        c.wait_send()
    for c in outs:
        c.wait()


def dot_0(a, b):
    return lax.dot_general(a, b, (((0,), (0,)), ((), ())), preferred_element_type=f32)


def denominator(en, p):
    across = jnp.broadcast_to(en[pl.ds(p, 1), :], (128, 128))
    return jnp.transpose(across) + across


def integrals(occ, cnt, eo, lists, en, factors, vecs):
    smem = pl.BlockSpec(memory_space=pltpu.SMEM)
    vmem = pl.BlockSpec(memory_space=pltpu.VMEM)
    anyw = pl.BlockSpec(memory_space=pl.ANY)
    i32 = jnp.int32
    dma = pltpu.SemaphoreType.DMA
    return pl.pallas_call(
        integral_kernel,
        out_shape=(
            jax.ShapeDtypeStruct((NP, 128, 128), f32),
            jax.ShapeDtypeStruct((NI, 1, 128), i32),
            jax.ShapeDtypeStruct((NJ, 1, 128), i32),
            jax.ShapeDtypeStruct((8, 128), i32),
            jax.ShapeDtypeStruct((1, 128), f32),
        ),
        in_specs=[smem] * 3 + [vmem] * 9 + [anyw] * 2,
        out_specs=(anyw, vmem, vmem, vmem, vmem),
        scratch_shapes=[
            pltpu.VMEM((NJ, ROWS, 256), f32),
            pltpu.VMEM((NJ, ROWS, 256), f32),
            pltpu.VMEM((NI, ROWS, 256), f32),
            pltpu.VMEM((NI, ROWS, 256), f32),
            *[pltpu.VMEM((NJ, ROWS, 256), bf16)] * 4,
            *[pltpu.VMEM((NI, ROWS, 256), bf16)] * 4,
            pltpu.VMEM((NP, 256, 128), f32),
            pltpu.VMEM((NP, 256, 256), bf16),
            pltpu.VMEM((NP, 128, 128), f32),
            pltpu.VMEM((8, 128), f32),
            pltpu.VMEM((NI, 1, 128), i32),
            pltpu.VMEM((NJ, 1, 128), i32),
            dma((5,)),
            dma((2, 22)),
            dma((WAVES, 2, 20)),
            dma((WAVES, 2, 20)),
            dma((WAVES, 8)),
            dma((WAVES, 8)),
            dma((4,)),
        ],
        compiler_params=pltpu.CompilerParams(collective_id=0, has_side_effects=True, vmem_limit_bytes=VMEM_ALL),
    )(occ, cnt, eo, *lists, en, factors, vecs)


UNROLL = 8
SLOTS = NI * CAPI + NJ * CAPJ


def couple(plan, weight, corr, arrived, term, ready=None):
    term[NC] = jnp.zeros((128, 128), f32)

    def body(b, run):
        places = [b * UNROLL + k for k in range(UNROLL)]
        if ready is not None:
            ready(places)
        corrs = [split(corr[plan[0, s]]) for s in places]
        stage = []
        for s, (mh, ml) in zip(places, corrs):
            xh, xl = split(arrived[plan[1, s] if ready is None else s])
            xx = jnp.concatenate([xh, xl], axis=1)
            stage.append((jnp.concatenate([mh, ml], axis=1), jnp.concatenate([xx, xx], axis=0)))
        stage = [dot(m, x) for m, x in stage]
        stage = [jnp.concatenate(split(h[:, :128] + h[:, 128:]), axis=1) for h in stage]
        corrs = [
            jnp.concatenate([jnp.concatenate([mh, mh], axis=1), jnp.concatenate([ml, ml], axis=1)], axis=0)
            for mh, ml in corrs
        ]
        stage = [dot_t(h, m) for h, m in zip(stage, corrs)]
        for s, t in zip(places, stage):
            t = (t[:, :128] + t[:, 128:]) * weight[0, s]
            run = jnp.where(plan[2, s] > 0, run, 0.0) + t
            term[s] = run
        return run

    lax.fori_loop(0, NC // UNROLL, body, jnp.zeros((128, 128), f32))


def iterate_kernel(
    qi, qj, plan, weight, occ, cnt, eo, en, amp0, ci, cj, amp_out, inv_out, held,
    amp, inv, corr, delta, term, snd_i, snd_j, mid, rcv0, mine, ls, hs, si, ri, sj, rj,
):
    u = lax.axis_index("occi")
    v = lax.axis_index("occj")
    x, z = v % 4, v // 4
    rows = lax.broadcasted_iota(jnp.int32, (128, 128), 0)
    cols = lax.broadcasted_iota(jnp.int32, (128, 128), 1)
    loads = [
        pltpu.make_async_copy(amp0, amp, ls.at[0]),
        pltpu.make_async_copy(ci, corr.at[pl.ds(0, 32)], ls.at[1]),
        pltpu.make_async_copy(cj, corr.at[pl.ds(32, 32)], ls.at[2]),
    ]
    for c in loads:
        c.start()
    greet(u, v)

    def vid(dz, dx):
        return ((z + dz) % 4) * 4 + (x + dx) % 4

    def exchange(it, src, arrived, beside):
        half_rows = CAPJ // 2
        first, rest, sent, kept = {}, [], [], []

        def fill(half, d):
            for e in range(4):
                if d == 0 and e == 0:
                    continue
                to = vid(e, d) if half == 0 else vid(d, e)
                for s in range(half_rows):
                    snd_j[it, half, d, half_rows * e + s] = src[qj[to, 0, half_rows * half + s]]

        def place(half, d, e):
            frm = vid((4 - e) % 4, (4 - d) % 4) if half == 0 else vid((4 - d) % 4, (4 - e) % 4)
            return arrived.at[pl.ds(NI * CAPI + frm * CAPJ + half_rows * half, half_rows)]

        for d in (2, 1, 3):
            for half in (0, 1):
                fill(half, d)
                to = vid(0, d) if half == 0 else vid(d, 0)
                c = pltpu.make_async_remote_copy(
                    snd_j.at[it, half, d], mid.at[it, half, d], sj.at[it, half, d, 0], rj.at[it, half, d, 0], {"occj": to}, MESH
                )
                c.start()
                first[half, d] = c
                sent.append(c)
        for k, off in enumerate(OFF_I):
            to, frm = peer_i(u, off), peer_i(u, back(off, (4, 2)))
            for s in range(CAPI):
                snd_i[it, k * CAPI + s] = src[qi[to, 0, s]]
            out = snd_i.at[it, pl.ds(k * CAPI, CAPI)]
            c = pltpu.make_async_remote_copy(
                out, arrived.at[pl.ds(u * CAPI, CAPI)], si.at[it, k], ri.at[it, k], {"occi": to}, MESH
            )
            c.start()
            sent.append(c)
            rest.append(
                pltpu.make_async_remote_copy(
                    out, arrived.at[pl.ds(frm * CAPI, CAPI)], si.at[it, k], ri.at[it, k], {"occi": to}, MESH
                )
            )

        def onward(half, d):
            for e in (2, 1, 3):
                to = vid(e, 0) if half == 0 else vid(0, e)
                out = (snd_j if d == 0 else mid).at[it, half, d, pl.ds(half_rows * e, half_rows)]
                start = vid(0, (4 - d) % 4) if half == 0 else vid((4 - d) % 4, 0)
                into = arrived.at[pl.ds(NI * CAPI + start * CAPJ + half_rows * half, half_rows)]
                c = pltpu.make_async_remote_copy(
                    out, into, sj.at[it, half, d, e], rj.at[it, half, d, e], {"occj": to}, MESH
                )
                c.start()
                sent.append(c)
                rest.append(
                    pltpu.make_async_remote_copy(
                        out, place(half, d, e), sj.at[it, half, d, e], rj.at[it, half, d, e], {"occj": to}, MESH
                    )
                )

        for half in (0, 1):
            fill(half, 0)
            onward(half, 0)
        stay = []
        for s in range(CAPI):
            mine[s] = src[qi[u, 0, s]]
        for s in range(CAPJ):
            mine[CAPI + s] = src[qj[v, 0, s]]
        stay.append((mine.at[pl.ds(0, CAPI)], u * CAPI, CAPI))
        stay.append((mine.at[pl.ds(CAPI, CAPJ)], NI * CAPI + v * CAPJ, CAPJ))
        for n, (a, at, size) in enumerate(stay):
            c = pltpu.make_async_copy(a, arrived.at[pl.ds(at, size)], hs.at[it, n])
            c.start()
            kept.append(c)
        beside(0)
        for d in (1, 3, 2):
            for half in (0, 1):
                first[half, d].wait_recv()
                onward(half, d)
            if d == 3:
                beside(1)
        for half in (0, 1):
            for d in (1, 3, 2):
                frm = vid(0, (4 - d) % 4) if half == 0 else vid((4 - d) % 4, 0)
                c = pltpu.make_async_copy(
                    mid.at[it, half, d, pl.ds(0, half_rows)],
                    arrived.at[pl.ds(NI * CAPI + frm * CAPJ + half_rows * half, half_rows)],
                    hs.at[it, 2 + 4 * half + d],
                )
                c.start()
                kept.append(c)
        beside(2)
        for c in rest:
            c.wait_recv()
        for c in sent:
            c.wait_send()
        for c in kept:
            c.wait()

    def inverses(lo, hi):
        def body(p, carry):
            den = denominator(en, p) - (eo[occ[0, p]] + eo[occ[1, p]])
            n = cnt[p]
            inv[p] = jnp.where((rows < n) & (cols < n), 1.0 / den, 0.0)
            return carry

        lax.fori_loop(lo, hi, body, 0)

    def beside0(part):
        if part == 0:
            inverses(0, 16)
        elif part == 1:
            inverses(16, 32)
        else:
            inverses(32, 64)
            for c in loads[1:]:
                c.wait()

    loads[0].wait()
    exchange(0, amp, rcv0, beside0)
    couple(plan, weight, corr, rcv0, term)

    def first(b, carry):
        for k in range(4):
            p = 4 * b + k
            delta[p] = term[plan[3, p]] * inv[p]
        return carry

    lax.fori_loop(0, NP // 4, first, 0)

    outs = [pltpu.make_async_copy(amp, amp_out, ls.at[3]), pltpu.make_async_copy(inv, inv_out, ls.at[4])]

    def beside1(part):
        if part == 0:
            outs[1].start()
        elif part == 1:

            def add(b, carry):
                for k in range(4):
                    p = 4 * b + k
                    amp[p] = amp[p] + delta[p]
                return carry

            lax.fori_loop(0, NP // 4, add, 0)
            outs[0].start()

    exchange(1, delta, held, beside1)
    for c in outs:
        c.wait()


def finish_kernel(plan, weight, cnt, amp0, inv0, held, ci, cj, amp_out, res_out, amp, inv, corr, arrived, term, ls, cs, gs, os):
    loads = [pltpu.make_async_copy(amp0, amp, ls.at[0]), pltpu.make_async_copy(inv0, inv, ls.at[1])]
    mats = [
        pltpu.make_async_copy(ci, corr.at[pl.ds(0, 32)], cs.at[0]),
        pltpu.make_async_copy(cj, corr.at[pl.ds(32, 32)], cs.at[1]),
    ]

    def fetch(s):
        return pltpu.make_async_copy(held.at[plan[1, s]], arrived.at[s], gs.at[s])

    def start(b, carry):
        for k in range(UNROLL):
            fetch(b * UNROLL + k).start()
        return carry

    def ready(places):
        for s in places:
            fetch(s).wait()

    lax.fori_loop(0, 1, start, 0)
    for c in mats:
        c.start()
    lax.fori_loop(1, NC // UNROLL, start, 0)
    for c in loads:
        c.start()
    for c in mats:
        c.wait()
    couple(plan, weight, corr, arrived, term, ready)
    for c in loads:
        c.wait()
    rows = lax.broadcasted_iota(jnp.int32, (128, 128), 0)
    cols = lax.broadcasted_iota(jnp.int32, (128, 128), 1)

    def second(b, carry):
        for k in range(4):
            p = 4 * b + k
            s = term[plan[3, p]]
            n = cnt[p]
            amp[p] = amp[p] + s * inv[p]
            inv[p] = jnp.where((rows < n) & (cols < n), -s, 0.0)
        return carry

    outs = []
    for k in range(4):
        lax.fori_loop(4 * k, 4 * k + 4, second, 0)
        part = pl.ds(16 * k, 16)
        outs.append(pltpu.make_async_copy(amp.at[part], amp_out.at[part], os.at[0, k]))
        outs.append(pltpu.make_async_copy(inv.at[part], res_out.at[part], os.at[1, k]))
        outs[-2].start()
        outs[-1].start()
    for c in outs:
        c.wait()


def finish(plan, weight, cnt, amp, inv, held, ci, cj):
    smem = pl.BlockSpec(memory_space=pltpu.SMEM)
    anyw = pl.BlockSpec(memory_space=pl.ANY)
    dma = pltpu.SemaphoreType.DMA
    mats = lambda *n: pltpu.VMEM(n + (128, 128), f32)
    return pl.pallas_call(
        finish_kernel,
        out_shape=(jax.ShapeDtypeStruct((NP, 128, 128), f32),) * 2,
        in_specs=[smem] * 3 + [anyw] * 5,
        out_specs=(anyw, anyw),
        scratch_shapes=[mats(NP), mats(NP), mats(NC), mats(NC), mats(NC + 1), dma((2,)), dma((2,)), dma((NC,)), dma((2, 4))],
        compiler_params=pltpu.CompilerParams(vmem_limit_bytes=VMEM_ALL),
    )(plan, weight, cnt, amp, inv, held, ci, cj)


def iterate(qi, qj, plan, weight, occ, cnt, eo, en, amp, ci, cj):
    smem = pl.BlockSpec(memory_space=pltpu.SMEM)
    vmem = pl.BlockSpec(memory_space=pltpu.VMEM)
    anyw = pl.BlockSpec(memory_space=pl.ANY)
    dma = pltpu.SemaphoreType.DMA
    mats = lambda *n: pltpu.VMEM(n + (128, 128), f32)
    return pl.pallas_call(
        iterate_kernel,
        out_shape=(jax.ShapeDtypeStruct((NP, 128, 128), f32),) * 2 + (jax.ShapeDtypeStruct((SLOTS, 128, 128), f32),),
        in_specs=[smem] * 7 + [vmem] + [anyw] * 3,
        out_specs=(anyw,) * 3,
        scratch_shapes=[
            mats(NP),
            mats(NP),
            mats(NC),
            mats(NP),
            mats(NC + 1),
            mats(2, 7 * CAPI),
            mats(2, 2, 4, 2 * CAPJ),
            mats(2, 2, 4, 2 * CAPJ),
            mats(SLOTS),
            mats(CAPI + CAPJ),
            dma((5,)),
            dma((2, 10)),
            dma((2, 7)),
            dma((2, 7)),
            dma((2, 2, 4, 4)),
            dma((2, 2, 4, 4)),
        ],
        compiler_params=pltpu.CompilerParams(collective_id=1, has_side_effects=True, vmem_limit_bytes=VMEM_ALL),
    )(qi, qj, plan, weight, occ, cnt, eo, en, amp, ci, cj)


def local(
    factors, pno_vecs, pair_occ, pno_count, pno_energy, occ_energy,
    coupi_peer, coupi_slot, coupi_target, coupi_fock, coupi_correlation,
    coupj_peer, coupj_slot, coupj_target, coupj_fock, coupj_correlation,
):
    lists = [
        a.reshape(1, 32)
        for a in (
            coupi_peer, coupj_peer, coupi_slot, coupj_slot, coupi_target, coupj_target, coupi_fock, coupj_fock,
        )
    ]
    occ = pair_occ.T
    amp, qi, qj, plan, weight = integrals(occ, pno_count, occ_energy, lists, pno_energy, factors, pno_vecs)
    amp, inv, held = iterate(
        qi, qj, plan, weight, occ, pno_count, occ_energy, pno_energy, amp, coupi_correlation, coupj_correlation
    )
    return finish(plan, weight, pno_count, amp, inv, held, coupi_correlation, coupj_correlation)


def solution(mesh):
    both = ("occi", "occj")
    three, two, one = P(both, None, None), P(both, None), P(both)
    placed = (
        three, three, two, one, two, P(),
        two, one, one, one, three,
        two, one, one, one, three,
    )
    return jax.shard_map(local, mesh=mesh, in_specs=placed, out_specs=(three, three), check_vma=False)
```

```python
import functools

import jax
import jax.numpy as jnp
from jax import lax
from jax.experimental import pallas as pl
from jax.experimental.pallas import tpu as pltpu
from jax.sharding import PartitionSpec as P

MESH = pl.DeviceIdType.MESH
f32 = jnp.float32
bf16 = jnp.bfloat16
NI, NJ = 8, 16
CAPI, CAPJ = 8, 4
NP = 64
NC = 64
SIZES = (192, 192, 128)
STARTS = (0, 192, 384)
WAVES = len(SIZES)
VMEM_ALL = 60 * 2**20
GROUP = 8

OFF_I = [(2, 0), (2, 1), (1, 0), (3, 0), (1, 1), (3, 1), (0, 1)]
OFF_J = sorted(
    [(a, b) for a in range(4) for b in range(4) if (a, b) != (0, 0)],
    key=lambda t: -(min(t[0], 4 - t[0]) + min(t[1], 4 - t[1])),
)


def split(x):
    hi = x.astype(bf16)
    return hi, (x - hi.astype(f32)).astype(bf16)


def dot(a, b):
    return jnp.dot(a, b, preferred_element_type=f32)


def dot_t(a, b):
    return lax.dot_general(a, b, (((1,), (1,)), ((), ())), preferred_element_type=f32)


def peer_i(u, off):
    return ((u // 2 + off[0]) % 4) * 2 + (u % 2 + off[1]) % 2


def peer_j(v, off):
    return ((v // 4 + off[0]) % 4) * 4 + (v % 4 + off[1]) % 4


def back(off, sizes):
    return tuple((n - o) % n for o, n in zip(off, sizes))


def greet(u, v):
    barrier = pltpu.get_barrier_semaphore()
    for off in OFF_I:
        pl.semaphore_signal(barrier, inc=1, device_id={"occi": peer_i(u, off)}, device_id_type=MESH)
    for off in OFF_J:
        pl.semaphore_signal(barrier, inc=1, device_id={"occj": peer_j(v, off)}, device_id_type=MESH)
    pl.semaphore_wait(barrier, len(OFF_I) + len(OFF_J))


def tables(tab, ri, rj, plan, weight):
    lane = lax.broadcasted_iota(jnp.int32, (NC, 128), 1)
    sub = lax.broadcasted_iota(jnp.int32, (NC, 128), 0)

    def across(r):
        return jnp.broadcast_to(tab[pl.ds(r, 1), :], (128, 128))

    def down(r):
        return jnp.transpose(across(r))[:NC]

    def count(mask, axis):
        return jnp.sum(jnp.where(mask, 1.0, 0.0), axis=axis, keepdims=True)

    def pick(mask, value):
        return jnp.sum(jnp.where(mask, value, 0.0), axis=0, keepdims=True)

    peer, slot, target, fock = down(0), down(1), down(2), down(3)
    rank = count((across(0)[:NC] == peer) & (lane < sub), 1)
    at = rank.astype(jnp.int32)
    for p in range(NI):
        ri[p] = pick((peer == p) & (at == lane), slot).astype(jnp.int32)
    for p in range(NJ):
        rj[p] = pick((peer == NI + p) & (at == lane), slot).astype(jnp.int32)
    arrival = jnp.where(peer < NI, peer * CAPI, NI * CAPI + (peer - NI) * CAPJ) + rank
    row_t = across(2)[:NC]
    equal = row_t == target
    place = count((row_t < target) | (equal & (lane < sub)), 1).astype(jnp.int32)
    goes_on = jnp.minimum(count(equal & (lane < sub), 1), 1.0)
    here = place == lane
    plan[pl.ds(0, 1), :] = pick(here, sub.astype(f32)).astype(jnp.int32)
    plan[pl.ds(1, 1), :] = pick(here, arrival).astype(jnp.int32)
    plan[pl.ds(2, 1), :] = pick(here, goes_on).astype(jnp.int32)
    lane_f = lane.astype(f32)
    upto = count(target <= lane_f, 0)
    plan[pl.ds(3, 1), :] = jnp.where(count(target == lane_f, 0) > 0.5, upto - 1.0, float(NC)).astype(jnp.int32)
    weight[...] = pick(here, fock)


def integral_kernel(
    occ, cnt, eo, pi, pj, si, sj, ti, tj, ki, kj, en, fac, vecs, amp, inv_out, qi, qj, plan, weight,
    fi, fj, th, tl, jh, jl, vec, both, acc, inv, tab, ri, rj, own_sem, tab_sem, rs, ss, crs, css, out_sem,
):
    u = lax.axis_index("occi")
    v = lax.axis_index("occj")
    x, z = v % 4, v // 4
    y, core = u // 2, u % 2

    def vid(zz, xx):
        return ((z + zz) % 4) * 4 + (x + xx) % 4

    def uid(yy, cc):
        return ((y + yy) % 4) * 2 + (core + cc) % 2

    own = [pltpu.make_async_copy(vecs, vec, own_sem.at[0])]
    for w in range(WAVES):
        at = fac.at[0, pl.ds(STARTS[w], SIZES[w])]
        own.append(pltpu.make_async_copy(at, fi[w].at[v], own_sem.at[1 + 2 * w]))
        own.append(pltpu.make_async_copy(at, fj[w].at[u], own_sem.at[2 + 2 * w]))
    greet(u, v)
    for c in own:
        c.start()
    pending = []

    def send(w, from_fac, buf, slot, q, n, sem, dev):
        at = buf[w].at[slot, pl.ds(q, n)]
        src = fac.at[0, pl.ds(STARTS[w] + q, n)] if from_fac else at
        c = pltpu.make_async_remote_copy(src, at, sem[0], sem[1], dev, MESH)
        c.start()
        pending.append(c)

    def got(w, buf, slot, q, n, sem, dev):
        at = buf[w].at[slot, pl.ds(q, n)]
        pltpu.make_async_remote_copy(at, at, sem[0], sem[1], dev, MESH).wait_recv()

    def wave(w):
        size = SIZES[w]
        h = size // 2
        s = h // 2

        def sem(half, k):
            return ss.at[w, half, k], rs.at[w, half, k]

        def csem(k):
            return css.at[w, k], crs.at[w, k]

        halves = []
        for half in (0, 1):
            if half == 0:
                first = lambda d: {"occj": vid(0, d)}
                second = lambda d: {"occj": vid(d, 0)}
                slot = lambda a, b: vid(b, a)
            else:
                first = lambda d: {"occj": vid(d, 0)}
                second = lambda d: {"occj": vid(0, d)}
                slot = lambda a, b: vid(a, b)
            halves.append((half, half * h, first, second, slot))

        def second_send(half, q, second, slot, a, base, mine=False):
            send(w, mine, fi, slot(a, 0), q, h, sem(half, base), second(1))
            send(w, mine, fi, slot(a, 0), q, h, sem(half, base + 1), second(3))

        def second_forward(half, q, second, slot, a, base):
            got(w, fi, slot(a, 3), q, h, sem(half, base), second(1))
            send(w, False, fi, slot(a, 3), q, s, sem(half, base + 2), second(1))
            got(w, fi, slot(a, 1), q, h, sem(half, base + 1), second(1))
            send(w, False, fi, slot(a, 1), q + s, s, sem(half, base + 3), second(3))

        def s0():
            for half, q, first, second, slot in halves:
                send(w, True, fi, v, q, h, sem(half, 0), first(1))
                send(w, True, fi, v, q, h, sem(half, 1), first(3))
            for half, q, first, second, slot in halves:
                second_send(half, q, second, slot, 0, 4, True)
            send(w, True, fj, u, 0, size, csem(0), {"occi": uid(1, 0)})
            send(w, True, fj, u, 0, size, csem(1), {"occi": uid(3, 0)})
            send(w, True, fj, u, 0, size, csem(4), {"occi": uid(0, 1)})

        def s1():
            for half, q, first, second, slot in halves:
                got(w, fi, slot(3, 0), q, h, sem(half, 0), first(1))
                send(w, False, fi, slot(3, 0), q, s, sem(half, 2), first(1))
                got(w, fi, slot(1, 0), q, h, sem(half, 1), first(1))
                send(w, False, fi, slot(1, 0), q + s, s, sem(half, 3), first(3))
            for half, q, first, second, slot in halves:
                second_send(half, q, second, slot, 3, 8)
                second_send(half, q, second, slot, 1, 12)

        def s2():
            for half, q, first, second, slot in halves:
                second_forward(half, q, second, slot, 0, 4)
            n = size // 2
            got(w, fj, uid(3, 0), 0, size, csem(0), {"occi": uid(1, 0)})
            send(w, False, fj, uid(3, 0), 0, n, csem(2), {"occi": uid(1, 0)})
            send(w, False, fj, uid(3, 0), 0, size, csem(5), {"occi": uid(0, 1)})
            got(w, fj, uid(1, 0), 0, size, csem(1), {"occi": uid(1, 0)})
            send(w, False, fj, uid(1, 0), n, n, csem(3), {"occi": uid(3, 0)})
            send(w, False, fj, uid(1, 0), 0, size, csem(6), {"occi": uid(0, 1)})

        def s3():
            for half, q, first, second, slot in halves:
                got(w, fi, slot(2, 0), q, s, sem(half, 2), first(1))
                got(w, fi, slot(2, 0), q + s, s, sem(half, 3), first(1))
                second_send(half, q, second, slot, 2, 16)

        def s4():
            for half, q, first, second, slot in halves:
                second_forward(half, q, second, slot, 3, 8)
                second_forward(half, q, second, slot, 1, 12)
            n = size // 2
            got(w, fj, uid(2, 0), 0, n, csem(2), {"occi": uid(1, 0)})
            got(w, fj, uid(2, 0), n, n, csem(3), {"occi": uid(1, 0)})
            send(w, False, fj, uid(2, 0), 0, size, csem(7), {"occi": uid(0, 1)})

        def s5():
            for half, q, first, second, slot in halves:
                second_forward(half, q, second, slot, 2, 16)

        def s6():
            for half, q, first, second, slot in halves:
                for a, base in ((0, 4), (3, 8), (1, 12), (2, 16)):
                    got(w, fi, slot(a, 2), q, s, sem(half, base + 2), second(1))
                    got(w, fi, slot(a, 2), q + s, s, sem(half, base + 3), second(1))
            for k, yy in ((4, 0), (5, 3), (6, 1), (7, 2)):
                got(w, fj, uid(yy, 1), 0, size, csem(k), {"occi": uid(0, 1)})

        return s0, s1, s2, s3, s4, s5, s6

    def halve_i(w, blocks):
        for dz, dx in blocks:
            k = vid(dz, dx)
            th[w][k], tl[w][k] = split(fi[w][k])

    def halve_j(w):
        def body(k, c):
            jh[w][k], jl[w][k] = split(fj[w][k])
            return c

        lax.fori_loop(0, NI, body, 0)

    def halve_vectors():
        def body(b, c):
            for k in range(2):
                h, l = split(vec[2 * b + k])
                both[2 * b + k] = jnp.concatenate([h, l], axis=1)
            return c

        lax.fori_loop(0, NP // 2, body, 0)

    rows = lax.broadcasted_iota(jnp.int32, (128, 128), 0)
    cols = lax.broadcasted_iota(jnp.int32, (128, 128), 1)

    def inverses():
        def body(b, c):
            group = [4 * b + k for k in range(4)]
            sums = [denominator(en, p) for p in group]
            for p, den in zip(group, sums):
                n = cnt[p]
                den = den - (eo[occ[0, p]] + eo[occ[1, p]])
                inv[p] = jnp.where((rows < n) & (cols < n), 1.0 / den, 0.0)
            return c

        lax.fori_loop(0, NP // 4, body, 0)

    def some(w, lo, hi):
        def body(b, c):
            group = [b * GROUP + g for g in range(GROUP)]
            stage = []
            for p in group:
                i, j = lax.rem(occ[0, p], NJ), lax.div(occ[1, p], NJ)
                hl = both[p]
                h = hl[:, :128]
                one = dot(th[w][i], hl)
                left = one[:, :128] + one[:, 128:] + dot(tl[w][i], h)
                two = dot(jh[w][j], hl)
                right = two[:, :128] + two[:, 128:] + dot(jl[w][j], h)
                stage.append((left, right))
            stage = [
                (jnp.concatenate(split(left), axis=1), jnp.concatenate(split(right), axis=1)) for left, right in stage
            ]
            stage = [dot_0(left, right) for left, right in stage]
            stage = [(o[:128, :128] + o[:128, 128:]) + o[128:, :128] for o in stage]
            if w == 0:
                for p, o in zip(group, stage):
                    acc[p] = o
                return c
            if w < WAVES - 1:
                for p, o in zip(group, stage):
                    acc[p] = acc[p] + o
                return c
            for p, o in zip(group, stage):
                acc[p] = -(acc[p] + o) * inv[p]
            return c

        lax.fori_loop(lo // GROUP, hi // GROUP, body, 0)

    near = [(0, 0), (0, 1), (0, 3), (1, 0), (3, 0)]
    middle = [(1, 1), (1, 3), (3, 1), (3, 3)]
    far = [(0, 2), (2, 0), (1, 2), (3, 2), (2, 1), (2, 3), (2, 2)]
    a, b, c3 = wave(0), wave(1), wave(2)
    a[0]()
    for r, (one, two, fill) in enumerate(((pi, pj, -1.0), (si, sj, 0.0), (ti, tj, 1000.0), (ki, kj, 0.0))):
        tab[pl.ds(r, 1), :] = jnp.full((1, 128), fill, f32)
        tab[pl.ds(r, 1), 0:32] = one[...].astype(f32)
        tab[pl.ds(r, 1), 32:64] = two[...].astype(f32) + (float(NI) if r == 0 else 0.0)
    tables(tab, ri, rj, plan, weight)
    b[0]()
    waits = []
    for k, off in enumerate(OFF_I + OFF_J):
        if k < 7:
            to, frm, me, r, q, name = peer_i(u, off), peer_i(u, back(off, (4, 2))), u, ri, qi, "occi"
        else:
            to, frm, me, r, q, name = peer_j(v, off), peer_j(v, back(off, (4, 4))), v, rj, qj, "occj"
        c = pltpu.make_async_remote_copy(r.at[to], q.at[me], tab_sem.at[0, k], tab_sem.at[1, k], {name: to}, MESH)
        c.start()
        pending.append(c)
        waits.append(
            pltpu.make_async_remote_copy(r.at[frm], q.at[frm], tab_sem.at[0, k], tab_sem.at[1, k], {name: to}, MESH)
        )
    qi[u] = ri[u]
    qj[v] = rj[v]
    a[1]()
    a[2]()
    a[3]()
    own[0].wait()
    halve_vectors()
    b[1]()
    for c in own[1:]:
        c.wait()
    halve_i(0, near)
    a[4]()
    inverses()
    keep = pltpu.make_async_copy(inv, inv_out, out_sem.at[4])
    keep.start()
    halve_i(0, middle)
    a[5]()
    b[2]()
    halve_i(1, near)
    b[3]()
    c3[0]()
    a[6]()
    halve_i(0, far)
    halve_j(0)
    some(0, 0, 16)
    b[4]()
    some(0, 16, 32)
    b[5]()
    c3[1]()
    some(0, 32, 64)
    halve_i(1, middle)
    c3[2]()
    halve_i(2, near)
    c3[3]()
    b[6]()
    halve_i(1, far)
    halve_j(1)
    some(1, 0, 16)
    c3[4]()
    some(1, 16, 32)
    c3[5]()
    some(1, 32, 64)
    halve_i(2, middle)
    c3[6]()
    halve_i(2, far)
    halve_j(2)
    outs = [keep]
    for k in range(4):
        some(WAVES - 1, 16 * k, 16 * k + 16)
        part = pl.ds(16 * k, 16)
        c = pltpu.make_async_copy(acc.at[part], amp.at[part], out_sem.at[k])
        c.start()
        outs.append(c)
    for c in waits:
        c.wait_recv()
    for c in pending:
        c.wait_send()
    for c in outs:
        c.wait()


def dot_0(a, b):
    return lax.dot_general(a, b, (((0,), (0,)), ((), ())), preferred_element_type=f32)


def denominator(en, p):
    across = jnp.broadcast_to(en[pl.ds(p, 1), :], (128, 128))
    return jnp.transpose(across) + across


def integrals(occ, cnt, eo, lists, en, factors, vecs):
    smem = pl.BlockSpec(memory_space=pltpu.SMEM)
    vmem = pl.BlockSpec(memory_space=pltpu.VMEM)
    anyw = pl.BlockSpec(memory_space=pl.ANY)
    i32 = jnp.int32
    dma = pltpu.SemaphoreType.DMA
    return pl.pallas_call(
        integral_kernel,
        out_shape=(
            jax.ShapeDtypeStruct((NP, 128, 128), f32),
            jax.ShapeDtypeStruct((NP, 128, 128), f32),
            jax.ShapeDtypeStruct((NI, 1, 128), i32),
            jax.ShapeDtypeStruct((NJ, 1, 128), i32),
            jax.ShapeDtypeStruct((8, 128), i32),
            jax.ShapeDtypeStruct((1, 128), f32),
        ),
        in_specs=[smem] * 3 + [vmem] * 9 + [anyw] * 2,
        out_specs=(anyw, anyw, vmem, vmem, vmem, vmem),
        scratch_shapes=[
            [pltpu.VMEM((NJ, n, 256), f32) for n in SIZES],
            [pltpu.VMEM((NI, n, 256), f32) for n in SIZES],
            [pltpu.VMEM((NJ, n, 256), bf16) for n in SIZES],
            [pltpu.VMEM((NJ, n, 256), bf16) for n in SIZES],
            [pltpu.VMEM((NI, n, 256), bf16) for n in SIZES],
            [pltpu.VMEM((NI, n, 256), bf16) for n in SIZES],
            pltpu.VMEM((NP, 256, 128), f32),
            pltpu.VMEM((NP, 256, 256), bf16),
            pltpu.VMEM((NP, 128, 128), f32),
            pltpu.VMEM((NP, 128, 128), f32),
            pltpu.VMEM((8, 128), f32),
            pltpu.VMEM((NI, 1, 128), i32),
            pltpu.VMEM((NJ, 1, 128), i32),
            dma((1 + 2 * WAVES,)),
            dma((2, 22)),
            dma((WAVES, 2, 20)),
            dma((WAVES, 2, 20)),
            dma((WAVES, 8)),
            dma((WAVES, 8)),
            dma((5,)),
        ],
        compiler_params=pltpu.CompilerParams(collective_id=0, has_side_effects=True, vmem_limit_bytes=VMEM_ALL),
    )(occ, cnt, eo, *lists, en, factors, vecs)


UNROLL = 8
SLOTS = NI * CAPI + NJ * CAPJ


def couple(plan, weight, corr, arrived, term, ready=None):
    term[NC] = jnp.zeros((128, 128), f32)

    def body(b, run):
        places = [b * UNROLL + k for k in range(UNROLL)]
        if ready is not None:
            ready(places)
        corrs = [split(corr[plan[0, s]]) for s in places]
        stage = []
        for s, (mh, ml) in zip(places, corrs):
            xh, xl = split(arrived[plan[1, s] if ready is None else s])
            xx = jnp.concatenate([xh, xl], axis=1)
            stage.append((jnp.concatenate([mh, ml], axis=1), jnp.concatenate([xx, xx], axis=0)))
        stage = [dot(m, x) for m, x in stage]
        stage = [jnp.concatenate(split(h[:, :128] + h[:, 128:]), axis=1) for h in stage]
        corrs = [
            jnp.concatenate([jnp.concatenate([mh, mh], axis=1), jnp.concatenate([ml, ml], axis=1)], axis=0)
            for mh, ml in corrs
        ]
        stage = [dot_t(h, m) for h, m in zip(stage, corrs)]
        for s, t in zip(places, stage):
            t = (t[:, :128] + t[:, 128:]) * weight[0, s]
            run = jnp.where(plan[2, s] > 0, run, 0.0) + t
            term[s] = run
        return run

    lax.fori_loop(0, NC // UNROLL, body, jnp.zeros((128, 128), f32))


def iterate_kernel(
    qi, qj, plan, weight, amp0, inv0, ci, cj, amp_out, held,
    amp, inv, corr, delta, term, snd_i, snd_j, mid, rcv0, mine, ls, hs, si, ri, sj, rj,
):
    u = lax.axis_index("occi")
    v = lax.axis_index("occj")
    x, z = v % 4, v // 4
    loads = [
        pltpu.make_async_copy(amp0, amp, ls.at[0]),
        pltpu.make_async_copy(ci, corr.at[pl.ds(0, 32)], ls.at[1]),
        pltpu.make_async_copy(cj, corr.at[pl.ds(32, 32)], ls.at[2]),
        pltpu.make_async_copy(inv0, inv, ls.at[4]),
    ]
    for c in loads:
        c.start()
    greet(u, v)

    def vid(dz, dx):
        return ((z + dz) % 4) * 4 + (x + dx) % 4

    def exchange(it, src, arrived, beside):
        half_rows = CAPJ // 2
        first, rest, sent, kept = {}, [], [], []

        def fill(half, d):
            for e in range(4):
                if d == 0 and e == 0:
                    continue
                to = vid(e, d) if half == 0 else vid(d, e)
                for s in range(half_rows):
                    snd_j[it, half, d, half_rows * e + s] = src[qj[to, 0, half_rows * half + s]]

        def place(half, d, e):
            frm = vid((4 - e) % 4, (4 - d) % 4) if half == 0 else vid((4 - d) % 4, (4 - e) % 4)
            return arrived.at[pl.ds(NI * CAPI + frm * CAPJ + half_rows * half, half_rows)]

        for d in (2, 1, 3):
            for half in (0, 1):
                fill(half, d)
                to = vid(0, d) if half == 0 else vid(d, 0)
                c = pltpu.make_async_remote_copy(
                    snd_j.at[it, half, d], mid.at[it, half, d], sj.at[it, half, d, 0], rj.at[it, half, d, 0], {"occj": to}, MESH
                )
                c.start()
                first[half, d] = c
                sent.append(c)
        for k, off in enumerate(OFF_I):
            to, frm = peer_i(u, off), peer_i(u, back(off, (4, 2)))
            for s in range(CAPI):
                snd_i[it, k * CAPI + s] = src[qi[to, 0, s]]
            out = snd_i.at[it, pl.ds(k * CAPI, CAPI)]
            c = pltpu.make_async_remote_copy(
                out, arrived.at[pl.ds(u * CAPI, CAPI)], si.at[it, k], ri.at[it, k], {"occi": to}, MESH
            )
            c.start()
            sent.append(c)
            rest.append(
                pltpu.make_async_remote_copy(
                    out, arrived.at[pl.ds(frm * CAPI, CAPI)], si.at[it, k], ri.at[it, k], {"occi": to}, MESH
                )
            )

        def onward(half, d):
            for e in (2, 1, 3):
                to = vid(e, 0) if half == 0 else vid(0, e)
                out = (snd_j if d == 0 else mid).at[it, half, d, pl.ds(half_rows * e, half_rows)]
                start = vid(0, (4 - d) % 4) if half == 0 else vid((4 - d) % 4, 0)
                into = arrived.at[pl.ds(NI * CAPI + start * CAPJ + half_rows * half, half_rows)]
                c = pltpu.make_async_remote_copy(
                    out, into, sj.at[it, half, d, e], rj.at[it, half, d, e], {"occj": to}, MESH
                )
                c.start()
                sent.append(c)
                rest.append(
                    pltpu.make_async_remote_copy(
                        out, place(half, d, e), sj.at[it, half, d, e], rj.at[it, half, d, e], {"occj": to}, MESH
                    )
                )

        for half in (0, 1):
            fill(half, 0)
            onward(half, 0)
        stay = []
        for s in range(CAPI):
            mine[s] = src[qi[u, 0, s]]
        for s in range(CAPJ):
            mine[CAPI + s] = src[qj[v, 0, s]]
        stay.append((mine.at[pl.ds(0, CAPI)], u * CAPI, CAPI))
        stay.append((mine.at[pl.ds(CAPI, CAPJ)], NI * CAPI + v * CAPJ, CAPJ))
        for n, (a, at, size) in enumerate(stay):
            c = pltpu.make_async_copy(a, arrived.at[pl.ds(at, size)], hs.at[it, n])
            c.start()
            kept.append(c)
        beside(0)
        for d in (1, 3, 2):
            for half in (0, 1):
                first[half, d].wait_recv()
                onward(half, d)
            if d == 3:
                beside(1)
        for half in (0, 1):
            for d in (1, 3, 2):
                frm = vid(0, (4 - d) % 4) if half == 0 else vid((4 - d) % 4, 0)
                c = pltpu.make_async_copy(
                    mid.at[it, half, d, pl.ds(0, half_rows)],
                    arrived.at[pl.ds(NI * CAPI + frm * CAPJ + half_rows * half, half_rows)],
                    hs.at[it, 2 + 4 * half + d],
                )
                c.start()
                kept.append(c)
        beside(2)
        for c in rest:
            c.wait_recv()
        for c in sent:
            c.wait_send()
        for c in kept:
            c.wait()

    def beside0(part):
        if part == 2:
            for c in loads[1:]:
                c.wait()

    loads[0].wait()
    exchange(0, amp, rcv0, beside0)
    couple(plan, weight, corr, rcv0, term)

    def first(b, carry):
        for k in range(4):
            p = 4 * b + k
            delta[p] = term[plan[3, p]] * inv[p]
        return carry

    lax.fori_loop(0, NP // 4, first, 0)

    out = pltpu.make_async_copy(amp, amp_out, ls.at[3])

    def beside1(part):
        if part == 1:

            def add(b, carry):
                for k in range(4):
                    p = 4 * b + k
                    amp[p] = amp[p] + delta[p]
                return carry

            lax.fori_loop(0, NP // 4, add, 0)
            out.start()

    exchange(1, delta, held, beside1)
    out.wait()


def finish_kernel(plan, weight, cnt, amp0, inv0, held, ci, cj, amp_out, res_out, amp, inv, corr, arrived, term, ls, cs, gs, os):
    loads = [pltpu.make_async_copy(amp0, amp, ls.at[0]), pltpu.make_async_copy(inv0, inv, ls.at[1])]
    mats = [
        pltpu.make_async_copy(ci, corr.at[pl.ds(0, 32)], cs.at[0]),
        pltpu.make_async_copy(cj, corr.at[pl.ds(32, 32)], cs.at[1]),
    ]

    def fetch(s):
        return pltpu.make_async_copy(held.at[plan[1, s]], arrived.at[s], gs.at[s])

    def start(b, carry):
        for k in range(UNROLL):
            fetch(b * UNROLL + k).start()
        return carry

    def ready(places):
        for s in places:
            fetch(s).wait()

    lax.fori_loop(0, 1, start, 0)
    for c in mats:
        c.start()
    lax.fori_loop(1, NC // UNROLL, start, 0)
    for c in loads:
        c.start()
    for c in mats:
        c.wait()
    couple(plan, weight, corr, arrived, term, ready)
    for c in loads:
        c.wait()
    rows = lax.broadcasted_iota(jnp.int32, (128, 128), 0)
    cols = lax.broadcasted_iota(jnp.int32, (128, 128), 1)

    def second(b, carry):
        for k in range(4):
            p = 4 * b + k
            s = term[plan[3, p]]
            n = cnt[p]
            amp[p] = amp[p] + s * inv[p]
            inv[p] = jnp.where((rows < n) & (cols < n), -s, 0.0)
        return carry

    outs = []
    for k in range(4):
        lax.fori_loop(4 * k, 4 * k + 4, second, 0)
        part = pl.ds(16 * k, 16)
        outs.append(pltpu.make_async_copy(amp.at[part], amp_out.at[part], os.at[0, k]))
        outs.append(pltpu.make_async_copy(inv.at[part], res_out.at[part], os.at[1, k]))
        outs[-2].start()
        outs[-1].start()
    for c in outs:
        c.wait()


def finish(plan, weight, cnt, amp, inv, held, ci, cj):
    smem = pl.BlockSpec(memory_space=pltpu.SMEM)
    anyw = pl.BlockSpec(memory_space=pl.ANY)
    dma = pltpu.SemaphoreType.DMA
    mats = lambda *n: pltpu.VMEM(n + (128, 128), f32)
    return pl.pallas_call(
        finish_kernel,
        out_shape=(jax.ShapeDtypeStruct((NP, 128, 128), f32),) * 2,
        in_specs=[smem] * 3 + [anyw] * 5,
        out_specs=(anyw, anyw),
        scratch_shapes=[mats(NP), mats(NP), mats(NC), mats(NC), mats(NC + 1), dma((2,)), dma((2,)), dma((NC,)), dma((2, 4))],
        compiler_params=pltpu.CompilerParams(vmem_limit_bytes=VMEM_ALL),
    )(plan, weight, cnt, amp, inv, held, ci, cj)


def iterate(qi, qj, plan, weight, amp, inv, ci, cj):
    smem = pl.BlockSpec(memory_space=pltpu.SMEM)
    vmem = pl.BlockSpec(memory_space=pltpu.VMEM)
    anyw = pl.BlockSpec(memory_space=pl.ANY)
    dma = pltpu.SemaphoreType.DMA
    mats = lambda *n: pltpu.VMEM(n + (128, 128), f32)
    return pl.pallas_call(
        iterate_kernel,
        out_shape=(jax.ShapeDtypeStruct((NP, 128, 128), f32), jax.ShapeDtypeStruct((SLOTS, 128, 128), f32)),
        in_specs=[smem] * 4 + [anyw] * 4,
        out_specs=(anyw,) * 2,
        scratch_shapes=[
            mats(NP),
            mats(NP),
            mats(NC),
            mats(NP),
            mats(NC + 1),
            mats(2, 7 * CAPI),
            mats(2, 2, 4, 2 * CAPJ),
            mats(2, 2, 4, 2 * CAPJ),
            mats(SLOTS),
            mats(CAPI + CAPJ),
            dma((5,)),
            dma((2, 10)),
            dma((2, 7)),
            dma((2, 7)),
            dma((2, 2, 4, 4)),
            dma((2, 2, 4, 4)),
        ],
        compiler_params=pltpu.CompilerParams(collective_id=1, has_side_effects=True, vmem_limit_bytes=VMEM_ALL),
    )(qi, qj, plan, weight, amp, inv, ci, cj)


def local(
    factors, pno_vecs, pair_occ, pno_count, pno_energy, occ_energy,
    coupi_peer, coupi_slot, coupi_target, coupi_fock, coupi_correlation,
    coupj_peer, coupj_slot, coupj_target, coupj_fock, coupj_correlation,
):
    lists = [
        a.reshape(1, 32)
        for a in (
            coupi_peer, coupj_peer, coupi_slot, coupj_slot, coupi_target, coupj_target, coupi_fock, coupj_fock,
        )
    ]
    occ = pair_occ.T
    amp, inv, qi, qj, plan, weight = integrals(occ, pno_count, occ_energy, lists, pno_energy, factors, pno_vecs)
    amp, held = iterate(qi, qj, plan, weight, amp, inv, coupi_correlation, coupj_correlation)
    return finish(plan, weight, pno_count, amp, inv, held, coupi_correlation, coupj_correlation)


def solution(mesh):
    both = ("occi", "occj")
    three, two, one = P(both, None, None), P(both, None), P(both)
    placed = (
        three, three, two, one, two, P(),
        two, one, one, one, three,
        two, one, one, one, three,
    )
    return jax.shard_map(local, mesh=mesh, in_specs=placed, out_specs=(three, three), check_vma=False)
```

```python
import functools

import jax
import jax.numpy as jnp
from jax import lax
from jax.experimental import pallas as pl
from jax.experimental.pallas import tpu as pltpu
from jax.sharding import PartitionSpec as P

MESH = pl.DeviceIdType.MESH
f32 = jnp.float32
bf16 = jnp.bfloat16
NI, NJ = 8, 16
CAPI, CAPJ = 8, 4
NP = 64
NC = 64
SIZES = (192, 192, 128)
STARTS = (0, 192, 384)
WAVES = len(SIZES)
VMEM_ALL = 60 * 2**20
GROUP = 16

OFF_I = [(2, 0), (2, 1), (1, 0), (3, 0), (1, 1), (3, 1), (0, 1)]
OFF_J = sorted(
    [(a, b) for a in range(4) for b in range(4) if (a, b) != (0, 0)],
    key=lambda t: -(min(t[0], 4 - t[0]) + min(t[1], 4 - t[1])),
)


def split(x):
    hi = x.astype(bf16)
    return hi, (x - hi.astype(f32)).astype(bf16)


def dot(a, b):
    return jnp.dot(a, b, preferred_element_type=f32)


def dot_t(a, b):
    return lax.dot_general(a, b, (((1,), (1,)), ((), ())), preferred_element_type=f32)


def peer_i(u, off):
    return ((u // 2 + off[0]) % 4) * 2 + (u % 2 + off[1]) % 2


def peer_j(v, off):
    return ((v // 4 + off[0]) % 4) * 4 + (v % 4 + off[1]) % 4


def back(off, sizes):
    return tuple((n - o) % n for o, n in zip(off, sizes))


def greet(u, v):
    barrier = pltpu.get_barrier_semaphore()
    for off in OFF_I:
        pl.semaphore_signal(barrier, inc=1, device_id={"occi": peer_i(u, off)}, device_id_type=MESH)
    for off in OFF_J:
        pl.semaphore_signal(barrier, inc=1, device_id={"occj": peer_j(v, off)}, device_id_type=MESH)
    pl.semaphore_wait(barrier, len(OFF_I) + len(OFF_J))


def tables(tab, ri, rj, plan, weight):
    lane = lax.broadcasted_iota(jnp.int32, (NC, 128), 1)
    sub = lax.broadcasted_iota(jnp.int32, (NC, 128), 0)

    def across(r):
        return jnp.broadcast_to(tab[pl.ds(r, 1), :], (128, 128))

    def down(r):
        return jnp.transpose(across(r))[:NC]

    def count(mask, axis):
        return jnp.sum(jnp.where(mask, 1.0, 0.0), axis=axis, keepdims=True)

    def pick(mask, value):
        return jnp.sum(jnp.where(mask, value, 0.0), axis=0, keepdims=True)

    peer, slot, target, fock = down(0), down(1), down(2), down(3)
    rank = count((across(0)[:NC] == peer) & (lane < sub), 1)
    at = rank.astype(jnp.int32)
    for p in range(NI):
        ri[p] = pick((peer == p) & (at == lane), slot).astype(jnp.int32)
    for p in range(NJ):
        rj[p] = pick((peer == NI + p) & (at == lane), slot).astype(jnp.int32)
    arrival = jnp.where(peer < NI, peer * CAPI, NI * CAPI + (peer - NI) * CAPJ) + rank
    row_t = across(2)[:NC]
    equal = row_t == target
    place = count((row_t < target) | (equal & (lane < sub)), 1).astype(jnp.int32)
    goes_on = jnp.minimum(count(equal & (lane < sub), 1), 1.0)
    here = place == lane
    plan[pl.ds(0, 1), :] = pick(here, sub.astype(f32)).astype(jnp.int32)
    plan[pl.ds(1, 1), :] = pick(here, arrival).astype(jnp.int32)
    plan[pl.ds(2, 1), :] = pick(here, goes_on).astype(jnp.int32)
    lane_f = lane.astype(f32)
    upto = count(target <= lane_f, 0)
    plan[pl.ds(3, 1), :] = jnp.where(count(target == lane_f, 0) > 0.5, upto - 1.0, float(NC)).astype(jnp.int32)
    weight[...] = pick(here, fock)


def integral_kernel(
    occ, cnt, eo, pi, pj, si, sj, ti, tj, ki, kj, en, fac, vecs, amp, inv_out, qi, qj, plan, weight,
    fi, fj, th, tl, jh, jl, vec, both, acc, inv, tab, ri, rj, own_sem, tab_sem, rs, ss, crs, css, out_sem,
):
    u = lax.axis_index("occi")
    v = lax.axis_index("occj")
    x, z = v % 4, v // 4
    y, core = u // 2, u % 2

    def vid(zz, xx):
        return ((z + zz) % 4) * 4 + (x + xx) % 4

    def uid(yy, cc):
        return ((y + yy) % 4) * 2 + (core + cc) % 2

    own = [pltpu.make_async_copy(vecs, vec, own_sem.at[0])]
    for w in range(WAVES):
        at = fac.at[0, pl.ds(STARTS[w], SIZES[w])]
        own.append(pltpu.make_async_copy(at, fi[w].at[v], own_sem.at[1 + 2 * w]))
        own.append(pltpu.make_async_copy(at, fj[w].at[u], own_sem.at[2 + 2 * w]))
    greet(u, v)
    for c in own:
        c.start()
    pending = []

    def send(w, from_fac, buf, slot, q, n, sem, dev):
        at = buf[w].at[slot, pl.ds(q, n)]
        src = fac.at[0, pl.ds(STARTS[w] + q, n)] if from_fac else at
        c = pltpu.make_async_remote_copy(src, at, sem[0], sem[1], dev, MESH)
        c.start()
        pending.append(c)

    def got(w, buf, slot, q, n, sem, dev):
        at = buf[w].at[slot, pl.ds(q, n)]
        pltpu.make_async_remote_copy(at, at, sem[0], sem[1], dev, MESH).wait_recv()

    def wave(w):
        size = SIZES[w]
        h = size // 2
        s = h // 2

        def sem(half, k):
            return ss.at[w, half, k], rs.at[w, half, k]

        def csem(k):
            return css.at[w, k], crs.at[w, k]

        halves = []
        for half in (0, 1):
            if half == 0:
                first = lambda d: {"occj": vid(0, d)}
                second = lambda d: {"occj": vid(d, 0)}
                slot = lambda a, b: vid(b, a)
            else:
                first = lambda d: {"occj": vid(d, 0)}
                second = lambda d: {"occj": vid(0, d)}
                slot = lambda a, b: vid(a, b)
            halves.append((half, half * h, first, second, slot))

        def second_send(half, q, second, slot, a, base, mine=False):
            send(w, mine, fi, slot(a, 0), q, h, sem(half, base), second(1))
            send(w, mine, fi, slot(a, 0), q, h, sem(half, base + 1), second(3))

        def second_forward(half, q, second, slot, a, base):
            got(w, fi, slot(a, 3), q, h, sem(half, base), second(1))
            send(w, False, fi, slot(a, 3), q, s, sem(half, base + 2), second(1))
            got(w, fi, slot(a, 1), q, h, sem(half, base + 1), second(1))
            send(w, False, fi, slot(a, 1), q + s, s, sem(half, base + 3), second(3))

        def s0():
            for half, q, first, second, slot in halves:
                send(w, True, fi, v, q, h, sem(half, 0), first(1))
                send(w, True, fi, v, q, h, sem(half, 1), first(3))
            for half, q, first, second, slot in halves:
                second_send(half, q, second, slot, 0, 4, True)
            send(w, True, fj, u, 0, size, csem(0), {"occi": uid(1, 0)})
            send(w, True, fj, u, 0, size, csem(1), {"occi": uid(3, 0)})
            send(w, True, fj, u, 0, size, csem(4), {"occi": uid(0, 1)})

        def s1():
            for half, q, first, second, slot in halves:
                got(w, fi, slot(3, 0), q, h, sem(half, 0), first(1))
                send(w, False, fi, slot(3, 0), q, s, sem(half, 2), first(1))
                got(w, fi, slot(1, 0), q, h, sem(half, 1), first(1))
                send(w, False, fi, slot(1, 0), q + s, s, sem(half, 3), first(3))
            for half, q, first, second, slot in halves:
                second_send(half, q, second, slot, 3, 8)
                second_send(half, q, second, slot, 1, 12)

        def s2():
            for half, q, first, second, slot in halves:
                second_forward(half, q, second, slot, 0, 4)
            n = size // 2
            got(w, fj, uid(3, 0), 0, size, csem(0), {"occi": uid(1, 0)})
            send(w, False, fj, uid(3, 0), 0, n, csem(2), {"occi": uid(1, 0)})
            send(w, False, fj, uid(3, 0), 0, size, csem(5), {"occi": uid(0, 1)})
            got(w, fj, uid(1, 0), 0, size, csem(1), {"occi": uid(1, 0)})
            send(w, False, fj, uid(1, 0), n, n, csem(3), {"occi": uid(3, 0)})
            send(w, False, fj, uid(1, 0), 0, size, csem(6), {"occi": uid(0, 1)})

        def s3():
            for half, q, first, second, slot in halves:
                got(w, fi, slot(2, 0), q, s, sem(half, 2), first(1))
                got(w, fi, slot(2, 0), q + s, s, sem(half, 3), first(1))
                second_send(half, q, second, slot, 2, 16)

        def s4():
            for half, q, first, second, slot in halves:
                second_forward(half, q, second, slot, 3, 8)
                second_forward(half, q, second, slot, 1, 12)
            n = size // 2
            got(w, fj, uid(2, 0), 0, n, csem(2), {"occi": uid(1, 0)})
            got(w, fj, uid(2, 0), n, n, csem(3), {"occi": uid(1, 0)})
            send(w, False, fj, uid(2, 0), 0, size, csem(7), {"occi": uid(0, 1)})

        def s5():
            for half, q, first, second, slot in halves:
                second_forward(half, q, second, slot, 2, 16)

        def s6():
            for half, q, first, second, slot in halves:
                for a, base in ((0, 4), (3, 8), (1, 12), (2, 16)):
                    got(w, fi, slot(a, 2), q, s, sem(half, base + 2), second(1))
                    got(w, fi, slot(a, 2), q + s, s, sem(half, base + 3), second(1))
            for k, yy in ((4, 0), (5, 3), (6, 1), (7, 2)):
                got(w, fj, uid(yy, 1), 0, size, csem(k), {"occi": uid(0, 1)})

        return s0, s1, s2, s3, s4, s5, s6

    def halve_i(w, blocks):
        for dz, dx in blocks:
            k = vid(dz, dx)
            th[w][k], tl[w][k] = split(fi[w][k])

    def halve_j(w):
        def body(k, c):
            jh[w][k], jl[w][k] = split(fj[w][k])
            return c

        lax.fori_loop(0, NI, body, 0)

    def halve_vectors():
        def body(b, c):
            for k in range(2):
                h, l = split(vec[2 * b + k])
                both[2 * b + k] = jnp.concatenate([h, l], axis=1)
            return c

        lax.fori_loop(0, NP // 2, body, 0)

    rows = lax.broadcasted_iota(jnp.int32, (128, 128), 0)
    cols = lax.broadcasted_iota(jnp.int32, (128, 128), 1)

    def inverses():
        def body(b, c):
            group = [4 * b + k for k in range(4)]
            sums = [denominator(en, p) for p in group]
            for p, den in zip(group, sums):
                n = cnt[p]
                den = den - (eo[occ[0, p]] + eo[occ[1, p]])
                inv[p] = jnp.where((rows < n) & (cols < n), 1.0 / den, 0.0)
            return c

        lax.fori_loop(0, NP // 4, body, 0)

    def some(w, lo, hi):
        def body(b, c):
            group = [b * GROUP + g for g in range(GROUP)]
            stage = []
            for p in group:
                i, j = lax.rem(occ[0, p], NJ), lax.div(occ[1, p], NJ)
                hl = both[p]
                h = hl[:, :128]
                one = dot(th[w][i], hl)
                left = one[:, :128] + one[:, 128:] + dot(tl[w][i], h)
                two = dot(jh[w][j], hl)
                right = two[:, :128] + two[:, 128:] + dot(jl[w][j], h)
                stage.append((left, right))
            stage = [
                (jnp.concatenate(split(left), axis=1), jnp.concatenate(split(right), axis=1)) for left, right in stage
            ]
            stage = [dot_0(left, right) for left, right in stage]
            stage = [(o[:128, :128] + o[:128, 128:]) + o[128:, :128] for o in stage]
            if w == 0:
                for p, o in zip(group, stage):
                    acc[p] = o
                return c
            if w < WAVES - 1:
                for p, o in zip(group, stage):
                    acc[p] = acc[p] + o
                return c
            for p, o in zip(group, stage):
                acc[p] = -(acc[p] + o) * inv[p]
            return c

        lax.fori_loop(lo // GROUP, hi // GROUP, body, 0)

    near = [(0, 0), (0, 1), (0, 3), (1, 0), (3, 0)]
    middle = [(1, 1), (1, 3), (3, 1), (3, 3)]
    far = [(0, 2), (2, 0), (1, 2), (3, 2), (2, 1), (2, 3), (2, 2)]
    a, b, c3 = wave(0), wave(1), wave(2)
    a[0]()
    for r, (one, two, fill) in enumerate(((pi, pj, -1.0), (si, sj, 0.0), (ti, tj, 1000.0), (ki, kj, 0.0))):
        tab[pl.ds(r, 1), :] = jnp.full((1, 128), fill, f32)
        tab[pl.ds(r, 1), 0:32] = one[...].astype(f32)
        tab[pl.ds(r, 1), 32:64] = two[...].astype(f32) + (float(NI) if r == 0 else 0.0)
    tables(tab, ri, rj, plan, weight)
    b[0]()
    waits = []
    for k, off in enumerate(OFF_I + OFF_J):
        if k < 7:
            to, frm, me, r, q, name = peer_i(u, off), peer_i(u, back(off, (4, 2))), u, ri, qi, "occi"
        else:
            to, frm, me, r, q, name = peer_j(v, off), peer_j(v, back(off, (4, 4))), v, rj, qj, "occj"
        c = pltpu.make_async_remote_copy(r.at[to], q.at[me], tab_sem.at[0, k], tab_sem.at[1, k], {name: to}, MESH)
        c.start()
        pending.append(c)
        waits.append(
            pltpu.make_async_remote_copy(r.at[frm], q.at[frm], tab_sem.at[0, k], tab_sem.at[1, k], {name: to}, MESH)
        )
    qi[u] = ri[u]
    qj[v] = rj[v]
    a[1]()
    a[2]()
    a[3]()
    own[0].wait()
    halve_vectors()
    b[1]()
    for c in own[1:]:
        c.wait()
    halve_i(0, near)
    a[4]()
    inverses()
    keep = pltpu.make_async_copy(inv, inv_out, out_sem.at[4])
    keep.start()
    halve_i(0, middle)
    a[5]()
    b[2]()
    halve_i(1, near)
    b[3]()
    c3[0]()
    a[6]()
    halve_i(0, far)
    halve_j(0)
    some(0, 0, 16)
    b[4]()
    some(0, 16, 32)
    b[5]()
    c3[1]()
    some(0, 32, 64)
    halve_i(1, middle)
    c3[2]()
    halve_i(2, near)
    c3[3]()
    b[6]()
    halve_i(1, far)
    halve_j(1)
    some(1, 0, 16)
    c3[4]()
    some(1, 16, 32)
    c3[5]()
    some(1, 32, 64)
    halve_i(2, middle)
    c3[6]()
    halve_i(2, far)
    halve_j(2)
    outs = [keep]
    for k in range(4):
        some(WAVES - 1, 16 * k, 16 * k + 16)
        part = pl.ds(16 * k, 16)
        c = pltpu.make_async_copy(acc.at[part], amp.at[part], out_sem.at[k])
        c.start()
        outs.append(c)
    for c in waits:
        c.wait_recv()
    for c in pending:
        c.wait_send()
    for c in outs:
        c.wait()


def dot_0(a, b):
    return lax.dot_general(a, b, (((0,), (0,)), ((), ())), preferred_element_type=f32)


def denominator(en, p):
    across = jnp.broadcast_to(en[pl.ds(p, 1), :], (128, 128))
    return jnp.transpose(across) + across


def integrals(occ, cnt, eo, lists, en, factors, vecs):
    smem = pl.BlockSpec(memory_space=pltpu.SMEM)
    vmem = pl.BlockSpec(memory_space=pltpu.VMEM)
    anyw = pl.BlockSpec(memory_space=pl.ANY)
    i32 = jnp.int32
    dma = pltpu.SemaphoreType.DMA
    return pl.pallas_call(
        integral_kernel,
        out_shape=(
            jax.ShapeDtypeStruct((NP, 128, 128), f32),
            jax.ShapeDtypeStruct((NP, 128, 128), f32),
            jax.ShapeDtypeStruct((NI, 1, 128), i32),
            jax.ShapeDtypeStruct((NJ, 1, 128), i32),
            jax.ShapeDtypeStruct((8, 128), i32),
            jax.ShapeDtypeStruct((1, 128), f32),
        ),
        in_specs=[smem] * 3 + [vmem] * 9 + [anyw] * 2,
        out_specs=(anyw, anyw, vmem, vmem, vmem, vmem),
        scratch_shapes=[
            [pltpu.VMEM((NJ, n, 256), f32) for n in SIZES],
            [pltpu.VMEM((NI, n, 256), f32) for n in SIZES],
            [pltpu.VMEM((NJ, n, 256), bf16) for n in SIZES],
            [pltpu.VMEM((NJ, n, 256), bf16) for n in SIZES],
            [pltpu.VMEM((NI, n, 256), bf16) for n in SIZES],
            [pltpu.VMEM((NI, n, 256), bf16) for n in SIZES],
            pltpu.VMEM((NP, 256, 128), f32),
            pltpu.VMEM((NP, 256, 256), bf16),
            pltpu.VMEM((NP, 128, 128), f32),
            pltpu.VMEM((NP, 128, 128), f32),
            pltpu.VMEM((8, 128), f32),
            pltpu.VMEM((NI, 1, 128), i32),
            pltpu.VMEM((NJ, 1, 128), i32),
            dma((1 + 2 * WAVES,)),
            dma((2, 22)),
            dma((WAVES, 2, 20)),
            dma((WAVES, 2, 20)),
            dma((WAVES, 8)),
            dma((WAVES, 8)),
            dma((5,)),
        ],
        compiler_params=pltpu.CompilerParams(collective_id=0, has_side_effects=True, vmem_limit_bytes=VMEM_ALL),
    )(occ, cnt, eo, *lists, en, factors, vecs)


UNROLL = 16
SLOTS = NI * CAPI + NJ * CAPJ


def couple(plan, weight, corr, arrived, term, ready=None):
    term[NC] = jnp.zeros((128, 128), f32)

    def body(b, run):
        places = [b * UNROLL + k for k in range(UNROLL)]
        if ready is not None:
            ready(places)
        corrs = [split(corr[plan[0, s]]) for s in places]
        stage = []
        for s, (mh, ml) in zip(places, corrs):
            xh, xl = split(arrived[plan[1, s] if ready is None else s])
            xx = jnp.concatenate([xh, xl], axis=1)
            stage.append((jnp.concatenate([mh, ml], axis=1), jnp.concatenate([xx, xx], axis=0)))
        stage = [dot(m, x) for m, x in stage]
        stage = [jnp.concatenate(split(h[:, :128] + h[:, 128:]), axis=1) for h in stage]
        corrs = [
            jnp.concatenate([jnp.concatenate([mh, mh], axis=1), jnp.concatenate([ml, ml], axis=1)], axis=0)
            for mh, ml in corrs
        ]
        stage = [dot_t(h, m) for h, m in zip(stage, corrs)]
        for s, t in zip(places, stage):
            t = (t[:, :128] + t[:, 128:]) * weight[0, s]
            run = jnp.where(plan[2, s] > 0, run, 0.0) + t
            term[s] = run
        return run

    lax.fori_loop(0, NC // UNROLL, body, jnp.zeros((128, 128), f32))


def iterate_kernel(
    qi, qj, plan, weight, amp0, inv0, ci, cj, amp_out, held,
    amp, inv, corr, delta, term, snd_i, snd_j, mid, rcv0, mine, ls, hs, si, ri, sj, rj,
):
    u = lax.axis_index("occi")
    v = lax.axis_index("occj")
    x, z = v % 4, v // 4
    loads = [
        pltpu.make_async_copy(amp0, amp, ls.at[0]),
        pltpu.make_async_copy(ci, corr.at[pl.ds(0, 32)], ls.at[1]),
        pltpu.make_async_copy(cj, corr.at[pl.ds(32, 32)], ls.at[2]),
        pltpu.make_async_copy(inv0, inv, ls.at[4]),
    ]
    for c in loads:
        c.start()
    greet(u, v)

    def vid(dz, dx):
        return ((z + dz) % 4) * 4 + (x + dx) % 4

    def exchange(it, src, arrived, beside):
        half_rows = CAPJ // 2
        first, rest, sent, kept = {}, [], [], []

        def fill(half, d):
            for e in range(4):
                if d == 0 and e == 0:
                    continue
                to = vid(e, d) if half == 0 else vid(d, e)
                for s in range(half_rows):
                    snd_j[it, half, d, half_rows * e + s] = src[qj[to, 0, half_rows * half + s]]

        def place(half, d, e):
            frm = vid((4 - e) % 4, (4 - d) % 4) if half == 0 else vid((4 - d) % 4, (4 - e) % 4)
            return arrived.at[pl.ds(NI * CAPI + frm * CAPJ + half_rows * half, half_rows)]

        for d in (2, 1, 3):
            for half in (0, 1):
                fill(half, d)
                to = vid(0, d) if half == 0 else vid(d, 0)
                c = pltpu.make_async_remote_copy(
                    snd_j.at[it, half, d], mid.at[it, half, d], sj.at[it, half, d, 0], rj.at[it, half, d, 0], {"occj": to}, MESH
                )
                c.start()
                first[half, d] = c
                sent.append(c)
        for k, off in enumerate(OFF_I):
            to, frm = peer_i(u, off), peer_i(u, back(off, (4, 2)))
            for s in range(CAPI):
                snd_i[it, k * CAPI + s] = src[qi[to, 0, s]]
            out = snd_i.at[it, pl.ds(k * CAPI, CAPI)]
            c = pltpu.make_async_remote_copy(
                out, arrived.at[pl.ds(u * CAPI, CAPI)], si.at[it, k], ri.at[it, k], {"occi": to}, MESH
            )
            c.start()
            sent.append(c)
            rest.append(
                pltpu.make_async_remote_copy(
                    out, arrived.at[pl.ds(frm * CAPI, CAPI)], si.at[it, k], ri.at[it, k], {"occi": to}, MESH
                )
            )

        def onward(half, d):
            for e in (2, 1, 3):
                to = vid(e, 0) if half == 0 else vid(0, e)
                out = (snd_j if d == 0 else mid).at[it, half, d, pl.ds(half_rows * e, half_rows)]
                start = vid(0, (4 - d) % 4) if half == 0 else vid((4 - d) % 4, 0)
                into = arrived.at[pl.ds(NI * CAPI + start * CAPJ + half_rows * half, half_rows)]
                c = pltpu.make_async_remote_copy(
                    out, into, sj.at[it, half, d, e], rj.at[it, half, d, e], {"occj": to}, MESH
                )
                c.start()
                sent.append(c)
                rest.append(
                    pltpu.make_async_remote_copy(
                        out, place(half, d, e), sj.at[it, half, d, e], rj.at[it, half, d, e], {"occj": to}, MESH
                    )
                )

        for half in (0, 1):
            fill(half, 0)
            onward(half, 0)
        stay = []
        for s in range(CAPI):
            mine[s] = src[qi[u, 0, s]]
        for s in range(CAPJ):
            mine[CAPI + s] = src[qj[v, 0, s]]
        stay.append((mine.at[pl.ds(0, CAPI)], u * CAPI, CAPI))
        stay.append((mine.at[pl.ds(CAPI, CAPJ)], NI * CAPI + v * CAPJ, CAPJ))
        for n, (a, at, size) in enumerate(stay):
            c = pltpu.make_async_copy(a, arrived.at[pl.ds(at, size)], hs.at[it, n])
            c.start()
            kept.append(c)
        beside(0)
        for d in (1, 3, 2):
            for half in (0, 1):
                first[half, d].wait_recv()
                onward(half, d)
            if d == 3:
                beside(1)
        for half in (0, 1):
            for d in (1, 3, 2):
                frm = vid(0, (4 - d) % 4) if half == 0 else vid((4 - d) % 4, 0)
                c = pltpu.make_async_copy(
                    mid.at[it, half, d, pl.ds(0, half_rows)],
                    arrived.at[pl.ds(NI * CAPI + frm * CAPJ + half_rows * half, half_rows)],
                    hs.at[it, 2 + 4 * half + d],
                )
                c.start()
                kept.append(c)
        beside(2)
        for c in rest:
            c.wait_recv()
        for c in sent:
            c.wait_send()
        for c in kept:
            c.wait()

    def beside0(part):
        if part == 2:
            for c in loads[1:]:
                c.wait()

    loads[0].wait()
    exchange(0, amp, rcv0, beside0)
    couple(plan, weight, corr, rcv0, term)

    def first(b, carry):
        for k in range(4):
            p = 4 * b + k
            delta[p] = term[plan[3, p]] * inv[p]
        return carry

    lax.fori_loop(0, NP // 4, first, 0)

    out = pltpu.make_async_copy(amp, amp_out, ls.at[3])

    def beside1(part):
        if part == 1:

            def add(b, carry):
                for k in range(4):
                    p = 4 * b + k
                    amp[p] = amp[p] + delta[p]
                return carry

            lax.fori_loop(0, NP // 4, add, 0)
            out.start()

    exchange(1, delta, held, beside1)
    out.wait()


def finish_kernel(plan, weight, cnt, amp0, inv0, held, ci, cj, amp_out, res_out, amp, inv, corr, arrived, term, ls, cs, gs, os):
    loads = [pltpu.make_async_copy(amp0, amp, ls.at[0]), pltpu.make_async_copy(inv0, inv, ls.at[1])]
    mats = [
        pltpu.make_async_copy(ci, corr.at[pl.ds(0, 32)], cs.at[0]),
        pltpu.make_async_copy(cj, corr.at[pl.ds(32, 32)], cs.at[1]),
    ]

    def fetch(s):
        return pltpu.make_async_copy(held.at[plan[1, s]], arrived.at[s], gs.at[s])

    def start(b, carry):
        for k in range(UNROLL):
            fetch(b * UNROLL + k).start()
        return carry

    def ready(places):
        for s in places:
            fetch(s).wait()

    lax.fori_loop(0, 1, start, 0)
    for c in mats:
        c.start()
    lax.fori_loop(1, NC // UNROLL, start, 0)
    for c in loads:
        c.start()
    for c in mats:
        c.wait()
    couple(plan, weight, corr, arrived, term, ready)
    for c in loads:
        c.wait()
    rows = lax.broadcasted_iota(jnp.int32, (128, 128), 0)
    cols = lax.broadcasted_iota(jnp.int32, (128, 128), 1)

    def second(b, carry):
        for k in range(4):
            p = 4 * b + k
            s = term[plan[3, p]]
            n = cnt[p]
            amp[p] = amp[p] + s * inv[p]
            inv[p] = jnp.where((rows < n) & (cols < n), -s, 0.0)
        return carry

    outs = []
    for k in range(4):
        lax.fori_loop(4 * k, 4 * k + 4, second, 0)
        part = pl.ds(16 * k, 16)
        outs.append(pltpu.make_async_copy(amp.at[part], amp_out.at[part], os.at[0, k]))
        outs.append(pltpu.make_async_copy(inv.at[part], res_out.at[part], os.at[1, k]))
        outs[-2].start()
        outs[-1].start()
    for c in outs:
        c.wait()


def finish(plan, weight, cnt, amp, inv, held, ci, cj):
    smem = pl.BlockSpec(memory_space=pltpu.SMEM)
    anyw = pl.BlockSpec(memory_space=pl.ANY)
    dma = pltpu.SemaphoreType.DMA
    mats = lambda *n: pltpu.VMEM(n + (128, 128), f32)
    return pl.pallas_call(
        finish_kernel,
        out_shape=(jax.ShapeDtypeStruct((NP, 128, 128), f32),) * 2,
        in_specs=[smem] * 3 + [anyw] * 5,
        out_specs=(anyw, anyw),
        scratch_shapes=[mats(NP), mats(NP), mats(NC), mats(NC), mats(NC + 1), dma((2,)), dma((2,)), dma((NC,)), dma((2, 4))],
        compiler_params=pltpu.CompilerParams(vmem_limit_bytes=VMEM_ALL),
    )(plan, weight, cnt, amp, inv, held, ci, cj)


def iterate(qi, qj, plan, weight, amp, inv, ci, cj):
    smem = pl.BlockSpec(memory_space=pltpu.SMEM)
    vmem = pl.BlockSpec(memory_space=pltpu.VMEM)
    anyw = pl.BlockSpec(memory_space=pl.ANY)
    dma = pltpu.SemaphoreType.DMA
    mats = lambda *n: pltpu.VMEM(n + (128, 128), f32)
    return pl.pallas_call(
        iterate_kernel,
        out_shape=(jax.ShapeDtypeStruct((NP, 128, 128), f32), jax.ShapeDtypeStruct((SLOTS, 128, 128), f32)),
        in_specs=[smem] * 4 + [anyw] * 4,
        out_specs=(anyw,) * 2,
        scratch_shapes=[
            mats(NP),
            mats(NP),
            mats(NC),
            mats(NP),
            mats(NC + 1),
            mats(2, 7 * CAPI),
            mats(2, 2, 4, 2 * CAPJ),
            mats(2, 2, 4, 2 * CAPJ),
            mats(SLOTS),
            mats(CAPI + CAPJ),
            dma((5,)),
            dma((2, 10)),
            dma((2, 7)),
            dma((2, 7)),
            dma((2, 2, 4, 4)),
            dma((2, 2, 4, 4)),
        ],
        compiler_params=pltpu.CompilerParams(collective_id=1, has_side_effects=True, vmem_limit_bytes=VMEM_ALL),
    )(qi, qj, plan, weight, amp, inv, ci, cj)


def local(
    factors, pno_vecs, pair_occ, pno_count, pno_energy, occ_energy,
    coupi_peer, coupi_slot, coupi_target, coupi_fock, coupi_correlation,
    coupj_peer, coupj_slot, coupj_target, coupj_fock, coupj_correlation,
):
    lists = [
        a.reshape(1, 32)
        for a in (
            coupi_peer, coupj_peer, coupi_slot, coupj_slot, coupi_target, coupj_target, coupi_fock, coupj_fock,
        )
    ]
    occ = pair_occ.T
    amp, inv, qi, qj, plan, weight = integrals(occ, pno_count, occ_energy, lists, pno_energy, factors, pno_vecs)
    amp, held = iterate(qi, qj, plan, weight, amp, inv, coupi_correlation, coupj_correlation)
    return finish(plan, weight, pno_count, amp, inv, held, coupi_correlation, coupj_correlation)


def solution(mesh):
    both = ("occi", "occj")
    three, two, one = P(both, None, None), P(both, None), P(both)
    placed = (
        three, three, two, one, two, P(),
        two, one, one, one, three,
        two, one, one, one, three,
    )
    return jax.shard_map(local, mesh=mesh, in_specs=placed, out_specs=(three, three), check_vma=False)
```
